32 devices in a mesh: space: 8 (over z, x), vel: 4 (over y, core).
Axes of the slice: x: 2, y: 2, z: 4, core: 2. Of those that a mesh axis runs over, the one named last changes fastest.
Arguments:
- distribution: float32 [32, 32, 2, 4096], P('space', None, None, 'vel'), may hold values from 0.0004 to 1, as said below
- wall_mask: int32 [32, 2, 2], P('space'), may hold values 0 or 1
- grid_point: int32 [4096], P('vel'), may hold values from 0 to 4095, as said below
- mirror_slot: int32 [4096], P('vel'), may hold values from 0 to 4095, as said below
Outputs:
- swept: float32 [32, 32, 2, 4096], P('space', None, None, 'vel')
The draws below stay inside these ranges and needn't reach their ends.
Inputs may be any that keep to these rules, and one draw needn't show every extreme that they name: grid_point is a permutation of 0 .. 4095. mirror_slot is a permutation; slot mirror_slot[s] holds the velocity of slot s with its second component negated. `distribution`: every entry is positive.
All inputs are finite; a program needn't handle non-finite values. No bound on the sum of `wall_mask` on one device may be relied on, other than what follows from the above.
Results may differ from the reference program's by a relative error of at most 0.0003.
Values sent between devices are 32-bit elements; how exact they have to be, the bound alone decides.
A program may use at most 64 MiB of HBM per device.

```python
import math
import jax
import jax.numpy as jnp
from jax import lax

VS = 16
V = 4096
NY = 32
NZ = 2
NX = 32


def velocity_pairs(key):
    order = jax.random.permutation(jax.random.fold_in(key, 11), V).astype(jnp.int32)
    inverse = jnp.zeros((V,), jnp.int32).at[order].set(jnp.arange(V, dtype=jnp.int32))
    first = order // (VS * VS)
    quadratic_average = order // VS % VS
    third = order % VS
    mirrored = first * VS * VS + (VS - 1 - quadratic_average) * VS + third
    return (order, inverse[mirrored])


def draw_grid_point(key, part):
    return velocity_pairs(key)[0]


def draw_mirror_slot(key, part):
    return velocity_pairs(key)[1]


def draw_distribution(key, part):
    order = velocity_pairs(key)[0]
    spacing = 8.0 / VS
    half = (VS - 1) / 2.0
    first = ((order // (VS * VS)).astype(jnp.float32) - half) * spacing
    quadratic_average = ((order // VS % VS).astype(jnp.float32) - half) * spacing
    third = ((order % VS).astype(jnp.float32) - half) * spacing
    keys = jax.random.split(jax.random.fold_in(key, 23), 10)
    line = (NX, 1, 1, 1)
    direction = jnp.where(jax.random.uniform(keys[0], line) < 0.5, -1.0, 1.0)
    beam_speed = direction * jax.random.uniform(keys[1], line, minval=2.2, maxval=3.0)
    bulk_speed = -direction * jax.random.uniform(keys[2], line, minval=0.2, maxval=0.6)
    share = jax.random.uniform(keys[3], line, minval=0.15, maxval=0.3)
    beam_var = jax.random.uniform(keys[4], line, minval=0.15, maxval=0.3)
    bulk_var = jax.random.uniform(keys[5], line, minval=0.5, maxval=0.9)
    spread = jax.random.uniform(keys[6], line, minval=1.5, maxval=2.5)
    beam_part = share / jnp.sqrt(beam_var) * jnp.exp(-(first - beam_speed) ** 2 / (2.0 * beam_var))
    bulk_part = (1.0 - share) / jnp.sqrt(bulk_var) * jnp.exp(-(first - bulk_speed) ** 2 / (2.0 * bulk_var))
    across = jnp.exp(-(quadratic_average * quadratic_average + third * third) / (2.0 * spread))
    profile = 0.002 + 0.8 * (beam_part + bulk_part) * across
    full = (NX, NY, NZ, V)
    noise = jnp.exp(jax.random.uniform(keys[9], full, minval=math.log(0.4), maxval=0.0))
    return (profile * noise).astype(jnp.float32)


def plant(entries, rng, low, high):
    longest = entries.shape.index(max(entries.shape))
    spots = []
    for shift in (0, 1):
        where = [jax.random.randint(jax.random.fold_in(rng, axis), (), 0, length) for axis, length in enumerate(entries.shape)]
        where[longest] = (where[longest] + shift) % entries.shape[longest]
        spots.append(tuple(where))
    return entries.at[spots[0]].set(low).at[spots[1]].set(high)


def setup_inputs(seed: int = 0) -> dict:
    splits = jax.random.split(jax.random.key(seed), 5)
    distribution = draw_distribution(jax.random.fold_in(splits[4], 71), 0)
    wall_mask = plant((jax.random.randint(splits[1], (NX, 2, NZ), 0, 4) < 3).astype(jnp.int32), jax.random.fold_in(splits[1], 1), 0, 1)
    grid_point = draw_grid_point(jax.random.fold_in(splits[4], 71), 0)
    mirror_slot = draw_mirror_slot(jax.random.fold_in(splits[4], 71), 0)
    return dict(distribution=distribution, wall_mask=wall_mask, grid_point=grid_point, mirror_slot=mirror_slot)


stream_x = 40.0
stream_y = 0.15
stream_z = 0.05
relaxation_multiplier = 0.05
shear_power_index = 0.81
diffusivity_ratio = 2.0 / 3.0


def velocity_table(grid_point, side):
    spacing = 8.0 / side
    half = (side - 1) / 2.0
    first = (grid_point // (side * side)).astype(jnp.float32)
    quadratic_average = ((grid_point // side) % side).astype(jnp.float32)
    third = (grid_point % side).astype(jnp.float32)
    return jnp.stack([(first - half) * spacing, (quadratic_average - half) * spacing, (third - half) * spacing])


def equilibrium(phase_occupancy_line, xi, integration_coefficient):
    particle_concentration = integration_coefficient * jnp.sum(phase_occupancy_line, -1)
    flow = [integration_coefficient * jnp.sum(phase_occupancy_line * xi[k], -1) / particle_concentration for k in range(3)]
    peculiar = [xi[k] - flow[k][..., None] for k in range(3)]
    magnitude_square = peculiar[0] * peculiar[0] + peculiar[1] * peculiar[1] + peculiar[2] * peculiar[2]
    kinetic_heat_level = integration_coefficient * jnp.sum(magnitude_square * phase_occupancy_line, -1) / (3.0 * particle_concentration)
    heat = [0.5 * integration_coefficient * jnp.sum(peculiar[k] * magnitude_square * phase_occupancy_line, -1) for k in range(3)]
    thermal_level_group = kinetic_heat_level[..., None]
    particle_concentration_local = particle_concentration[..., None]
    gaussian_equilibrium = particle_concentration_local / (2.0 * math.pi * thermal_level_group) ** 1.5 * jnp.exp(-magnitude_square / (2.0 * thermal_level_group))
    lengthwise = peculiar[0] * heat[0][..., None] + peculiar[1] * heat[1][..., None] + peculiar[2] * heat[2][..., None]
    corrected_equilibrium = gaussian_equilibrium * (1.0 + (1.0 - diffusivity_ratio) * lengthwise / (5.0 * particle_concentration_local * thermal_level_group * thermal_level_group) * (magnitude_square / thermal_level_group - 5.0))
    relaxation_frequency = relaxation_multiplier * particle_concentration * kinetic_heat_level ** (1.0 - shear_power_index)
    return corrected_equilibrium, relaxation_frequency


def row_terms(phase_occupancy_line, mask_row, xi, mirror_slot, integration_coefficient):
    corrected_equilibrium, relaxation_frequency = equilibrium(phase_occupancy_line, xi, integration_coefficient)
    ghost_low = jnp.where(mask_row[0][:, None] == 1, phase_occupancy_line[0][:, mirror_slot], corrected_equilibrium[0])
    ghost_high = jnp.where(mask_row[1][:, None] == 1, phase_occupancy_line[-1][:, mirror_slot], corrected_equilibrium[-1])
    padded = jnp.concatenate([ghost_low[None], phase_occupancy_line, ghost_high[None]], axis=0)
    below = padded[:-2]
    above = padded[2:]
    y_flux = xi[1] * jnp.where(xi[1] > 0, phase_occupancy_line - below, above - phase_occupancy_line)
    z_flux = xi[2] * jnp.where(xi[2] > 0, phase_occupancy_line - jnp.roll(phase_occupancy_line, 1, axis=1), jnp.roll(phase_occupancy_line, -1, axis=1) - phase_occupancy_line)
    sigma = stream_x * jnp.abs(xi[0])
    denom = 1.0 + sigma + relaxation_frequency[..., None]
    coef_a = sigma / denom
    coef_b = (phase_occupancy_line + relaxation_frequency[..., None] * corrected_equilibrium - stream_y * y_flux - stream_z * z_flux) / denom
    return coef_a, coef_b


def reference(distribution, wall_mask, grid_point, mirror_slot):
    xi = velocity_table(grid_point, VS)
    integration_coefficient = (8.0 / VS) ** 3

    def one_row(pair):
        return row_terms(pair[0], pair[1], xi, mirror_slot, integration_coefficient)

    coef_a, coef_b = lax.map(one_row, (distribution, wall_mask))
    first_target = equilibrium(distribution[0], xi, integration_coefficient)[0]
    last_target = equilibrium(distribution[-1], xi, integration_coefficient)[0]

    def advance(prev, pair):
        value = pair[0] * prev + pair[1]
        return value, value

    downstream = lax.scan(advance, first_target, (coef_a, coef_b))[1]
    upstream = lax.scan(advance, last_target, (coef_a, coef_b), reverse=True)[1]
    return jnp.where(xi[0] > 0, downstream, upstream)
```

```python
import functools
import math

import jax
import jax.numpy as jnp
from jax import lax
from jax.experimental import pallas as pl
from jax.experimental.pallas import tpu as pltpu
from jax.sharding import PartitionSpec as P

VS = 16
LANE = 128
FEAT = 8
MOM = 16
MESH = pl.DeviceIdType.MESH

stream_x = 40.0
stream_y = 0.15
stream_z = 0.05
relaxation_multiplier = 0.05
shear_power_index = 0.81
diffusivity_ratio = 2.0 / 3.0

F32 = jnp.float32
BF16 = jnp.bfloat16


def rounded(x):
    return x.astype(BF16).astype(F32)


def velocity_rows(points):
    spacing = 8.0 / VS
    half = (VS - 1) / 2.0
    bits = VS.bit_length() - 1
    first = lax.shift_right_logical(points, 2 * bits).astype(F32)
    second = (lax.shift_right_logical(points, bits) & (VS - 1)).astype(F32)
    third = (points & (VS - 1)).astype(F32)
    return [(v - half) * spacing for v in (first, second, third)]


def stacked(rows, height):
    index = lax.broadcasted_iota(jnp.int32, (height, LANE), 0)
    out = jnp.zeros((height, LANE), F32)
    for k, row in enumerate(rows):
        out = jnp.where(index == k, row, out)
    return out


def kernel(
    dims,
    wall_mask,
    grid_ref,
    mirror_ref,
    f_hbm,
    out_ref,
    f_ref,
    wall_ref,
    whi_ref,
    wlo_ref,
    mirrored_ref,
    fhi_ref,
    flo_ref,
    tmom_ref,
    gmat_ref,
    mom_ref,
    coef_ref,
    lhs_ref,
    rate_ref,
    prate_ref,
    rate_send,
    rate_recv,
    sa_ref,
    sb_ref,
    pb_ref,
    pair_a,
    pair_b,
    ed_ref,
    eu_ref,
    od_ref,
    ou_ref,
    enter_own,
    enter_send,
    enter_recv,
    f_sem,
    wall_ssem,
    wall_rsem,
    mom_ssem,
    mom_rsem,
    rate_sem,
    face_ssem,
    face_rsem,
    dn_ssem,
    dn_rsem,
    up_ssem,
    up_rsem,
    ret_ssem,
    ret_rsem,
):
    depth, rows, planes, blocks, nspace, nvel = dims
    stride = blocks * planes
    pad = stride
    cells_x = planes * rows
    cells = depth * cells_x
    walls = depth * 2 * planes
    half_blocks = blocks // 2
    pairs = nspace // 2
    weight = (8.0 / VS) ** 3

    s = lax.axis_index("space")
    v = lax.axis_index("vel")
    q = lax.rem(s, 2)
    p = lax.div(s, 2)
    partner = s + 1 - 2 * q
    own0 = q * half_blocks
    far0 = (1 - q) * half_blocks

    def frow(x, y, j, z):
        return pad + (x * rows + y) * stride + j * planes + z

    load = pltpu.make_async_copy(f_hbm, f_ref.at[pl.ds(pad, depth * rows * stride)], f_sem)
    load.start()

    barrier = pltpu.get_barrier_semaphore()
    for d in range(1, nvel):
        pl.semaphore_signal(
            barrier, inc=1, device_id=(s, lax.rem(v + d, nvel)), device_id_type=MESH
        )
    pl.semaphore_signal(barrier, inc=1, device_id=(partner, v), device_id_type=MESH)

    @pl.when(p > 0)
    def _():
        pl.semaphore_signal(barrier, inc=1, device_id=(s - 2, v), device_id_type=MESH)

    @pl.when(p < pairs - 1)
    def _():
        pl.semaphore_signal(barrier, inc=1, device_id=(s + 2, v), device_id_type=MESH)

    tmom_ref[...] = jnp.zeros_like(tmom_ref)
    gmat_ref[...] = jnp.zeros_like(gmat_ref)
    coef_ref[...] = jnp.zeros_like(coef_ref)
    f_ref[pl.ds(0, pad)] = jnp.zeros((pad, LANE), F32)
    f_ref[pl.ds(pad + depth * rows * stride, pad)] = jnp.zeros((pad, LANE), F32)
    for j in range(blocks):
        x1, x2, x3 = velocity_rows(grid_ref[j : j + 1, :])
        one = jnp.ones_like(x1)
        square = x1 * x1 + x2 * x2 + x3 * x3
        cubic = [x * square for x in (x1, x2, x3)]
        cubic_hi = [rounded(x) for x in cubic]
        cubic_lo = [x - h for x, h in zip(cubic, cubic_hi)]
        table = [one, x1, x2, x3, x1 * x1, x2 * x2, x3 * x3, x1 * x2, x1 * x3, x2 * x3]
        tmom_ref[0:MOM, j * LANE : (j + 1) * LANE] = stacked(
            table + cubic_hi + cubic_lo, MOM
        ).astype(BF16)
        feat = stacked(table[:7], FEAT)
        zero = jnp.zeros_like(feat)
        for g in range(3):
            column = [zero] * 9
            for part in range(3):
                column[3 * part + g] = feat
            column = column + [zero]
            gmat_ref[j, 0 : 10 * FEAT, g * LANE : (g + 1) * LANE] = jnp.concatenate(
                column, axis=0
            ).astype(BF16)

    load.wait()

    for x in range(depth):
        for w in range(2):
            for z in range(planes):
                r = (x * 2 + w) * planes + z
                y = (rows - 1) * w
                wall_ref[v, pl.ds(r, blocks, stride=walls), :] = f_ref[
                    pl.ds(frow(x, y, 0, z), blocks, stride=planes), :
                ]

    greetings = nvel + (p > 0).astype(jnp.int32) + (p < pairs - 1).astype(jnp.int32)
    pl.semaphore_wait(barrier, greetings)

    def wall_copy(d):
        return pltpu.make_async_remote_copy(
            src_ref=wall_ref.at[v],
            dst_ref=wall_ref.at[v],
            send_sem=wall_ssem.at[d - 1],
            recv_sem=wall_rsem.at[d - 1],
            device_id=(s, lax.rem(v + d, nvel)),
            device_id_type=MESH,
        )

    def wall_arrival(d):
        origin = lax.rem(v + nvel - d, nvel)
        return pltpu.make_async_remote_copy(
            src_ref=wall_ref.at[origin],
            dst_ref=wall_ref.at[origin],
            send_sem=wall_ssem.at[d - 1],
            recv_sem=wall_rsem.at[d - 1],
            device_id=(s, lax.rem(v + d, nvel)),
            device_id_type=MESH,
        )

    def mom_copy(d):
        return pltpu.make_async_remote_copy(
            src_ref=mom_ref.at[0],
            dst_ref=mom_ref.at[d],
            send_sem=mom_ssem.at[d - 1],
            recv_sem=mom_rsem.at[d - 1],
            device_id=(s, lax.rem(v + d, nvel)),
            device_id_type=MESH,
        )

    for d in range(1, nvel):
        wall_copy(d).start()

    for x in range(depth):
        for z in range(planes):
            base = (x * planes + z) * rows
            for j in range(blocks):
                part = f_ref[pl.ds(frow(x, 0, j, z), rows, stride=stride), :]
                hi = part.astype(BF16)
                lo = (part - hi.astype(F32)).astype(BF16)
                fhi_ref[base : base + rows, j * LANE : (j + 1) * LANE] = hi
                flo_ref[base : base + rows, j * LANE : (j + 1) * LANE] = lo
    contract = (((1,), (1,)), ((), ()))
    sums = lax.dot_general(
        fhi_ref[...], tmom_ref[...], contract, preferred_element_type=F32
    ) + lax.dot_general(flo_ref[...], tmom_ref[...], contract, preferred_element_type=F32)
    mom_ref[0] = sums.T[0:MOM, :]
    for d in range(1, nvel):
        mom_copy(d).start()
    total = mom_ref[0]
    for d in range(1, nvel):
        mom_copy(d).wait_recv()
        total = total + mom_ref[d]
    total = total * weight

    raw = [total[k : k + 1, :] for k in range(MOM)]
    density = raw[0]
    momentum = raw[1:4]
    flow = [m / density for m in momentum]
    tensor = [[raw[4], raw[7], raw[8]], [raw[7], raw[5], raw[9]], [raw[8], raw[9], raw[6]]]
    third = [raw[10 + k] + raw[13 + k] for k in range(3)]
    trace = raw[4] + raw[5] + raw[6]
    flow_sq = flow[0] * flow[0] + flow[1] * flow[1] + flow[2] * flow[2]
    temperature = (trace - density * flow_sq) / (3.0 * density)
    flow_mom = flow[0] * momentum[0] + flow[1] * momentum[1] + flow[2] * momentum[2]
    heat = []
    for k in range(3):
        contracted = flow[0] * tensor[k][0] + flow[1] * tensor[k][1] + flow[2] * tensor[k][2]
        heat.append(
            0.5
            * (
                third[k]
                - 2.0 * contracted
                + flow_sq * momentum[k]
                - flow[k] * trace
                + 2.0 * flow[k] * flow_mom
                - flow[k] * flow_sq * density
            )
        )
    log_t = jnp.log(temperature)
    inverse_t = 1.0 / temperature
    rate = relaxation_multiplier * density * jnp.exp((1.0 - shear_power_index) * log_t)

    rate_send[...] = jnp.broadcast_to(rate, rate_send.shape)

    def rate_copy():
        return pltpu.make_async_remote_copy(
            src_ref=rate_send,
            dst_ref=rate_recv,
            send_sem=rate_sem.at[0],
            recv_sem=rate_sem.at[1],
            device_id=(partner, v),
            device_id_type=MESH,
        )

    rate_copy().start()
    scale = (1.0 - diffusivity_ratio) / 5.0 * inverse_t * inverse_t / density
    flow_heat = flow[0] * heat[0] + flow[1] * heat[1] + flow[2] * heat[2]
    exponent = [
        jnp.log(density) - 1.5 * (log_t + math.log(2.0 * math.pi)) - 0.5 * flow_sq * inverse_t
    ]
    exponent += [u * inverse_t for u in flow] + [-0.5 * inverse_t] * 3
    linear = [-scale * flow_heat] + [scale * h for h in heat]
    bracket = [flow_sq * inverse_t - 5.0]
    bracket += [-2.0 * u * inverse_t for u in flow] + [inverse_t] * 3
    for g, group in enumerate((exponent, linear, bracket)):
        for k, row in enumerate(group):
            coef_ref[g * FEAT + k : g * FEAT + k + 1, :] = row
    whole = coef_ref[0 : 3 * FEAT, :]
    hi = rounded(whole)
    mid = rounded(whole - hi)
    coef_ref[0 : 3 * FEAT, :] = hi
    coef_ref[3 * FEAT : 6 * FEAT, :] = mid
    coef_ref[6 * FEAT : 9 * FEAT, :] = whole - hi - mid
    lhs_ref[...] = coef_ref[...].T.astype(BF16)
    rate_ref[...] = jnp.broadcast_to(rate, (LANE, cells)).T

    for d in range(1, nvel):
        wall_arrival(d).wait_recv()
    everywhere = wall_ref[...].reshape(nvel * blocks * walls, LANE)
    whi = everywhere.astype(BF16)
    whi_ref[...] = whi
    wlo_ref[...] = (everywhere - whi.astype(F32)).astype(BF16)

    def mirror_block(j, carry):
        slot = mirror_ref[pl.ds(j, 1), :]
        low = slot & (LANE - 1)
        high = lax.shift_right_logical(slot, LANE.bit_length() - 1)
        lane_index = lax.broadcasted_iota(jnp.int32, (LANE, LANE), 0)
        pick = jnp.where(lane_index == low, 1.0, 0.0).astype(BF16)
        found = jnp.dot(whi_ref[...], pick, preferred_element_type=F32) + jnp.dot(
            wlo_ref[...], pick, preferred_element_type=F32
        )
        acc = jnp.zeros((walls, LANE), F32)
        for h in range(nvel * blocks):
            acc = acc + jnp.where(high == h, found[h * walls : (h + 1) * walls], 0.0)
        mirrored_ref[j] = acc
        return carry

    lax.fori_loop(0, blocks, mirror_block, 0)

    first_edge = jnp.where(s == 0, 1.0, 0.0).astype(F32)
    last_edge = jnp.where(s == nspace - 1, 1.0, 0.0).astype(F32)
    row_index = lax.broadcasted_iota(jnp.int32, (rows, LANE), 0)

    def block_tables(j):
        return velocity_rows(grid_ref[pl.ds(j, 1), :])

    def local_block(j):
        x1, x2, x3 = block_tables(j)
        pos1 = x1 > 0
        pos2 = x2 > 0
        pos3 = x3 > 0
        coef_y = stream_y * jnp.abs(x2)
        coef_z = stream_z * jnp.abs(x3)
        coef_f = 1.0 - coef_y - coef_z
        sigma = stream_x * jnp.abs(x1)
        opening = 1.0 + sigma
        edge = jnp.where(pos1, first_edge, last_edge)
        mirrored = mirrored_ref[j]
        a_list, b_list, eq_list = [], [], []
        for x in range(depth):
            base = x * cells_x
            got = jnp.dot(
                lhs_ref[base : base + cells_x, :], gmat_ref[j], preferred_element_type=F32
            )
            equilibrium = jnp.exp(got[:, :LANE]) * (
                1.0 + got[:, LANE : 2 * LANE] * got[:, 2 * LANE :]
            )
            rates = rate_ref[base : base + cells_x, :]
            inverse = 1.0 / (opening + rates)
            source = rates * equilibrium
            values = [
                f_ref[pl.ds(frow(x, 0, j, z), rows, stride=stride), :] for z in range(planes)
            ]
            parts = []
            for z in range(planes):
                low = (x * 2) * planes + z
                high = (x * 2 + 1) * planes + z
                mask_low = jnp.full((1, LANE), wall_mask[x, 0, z])
                mask_high = jnp.full((1, LANE), wall_mask[x, 1, z])
                eq_z = equilibrium[z * rows : (z + 1) * rows]
                ghost_low = jnp.where(mask_low == 1, mirrored[low : low + 1], eq_z[0:1])
                ghost_high = jnp.where(
                    mask_high == 1, mirrored[high : high + 1], eq_z[rows - 1 : rows]
                )
                below = f_ref[pl.ds(frow(x, -1, j, z), rows, stride=stride), :]
                above = f_ref[pl.ds(frow(x, 1, j, z), rows, stride=stride), :]
                below = jnp.where(row_index == 0, ghost_low, below)
                above = jnp.where(row_index == rows - 1, ghost_high, above)
                side = jnp.where(pos2, below, above)
                before, after = values[(z - 1) % planes], values[(z + 1) % planes]
                if (z - 1) % planes == (z + 1) % planes:
                    plane = before
                else:
                    plane = jnp.where(pos3, before, after)
                parts.append(coef_f * values[z] + coef_y * side + coef_z * plane)
            b_list.append((jnp.concatenate(parts, axis=0) + source) * inverse)
            a_list.append(sigma * inverse)
            if x in (0, depth - 1):
                eq_list.append(equilibrium)
        a_run = b_run = None
        for k in range(depth):
            a_k = jnp.where(pos1, a_list[k], a_list[depth - 1 - k])
            b_k = jnp.where(pos1, b_list[k], b_list[depth - 1 - k])
            if k == 0:
                target = jnp.where(pos1, eq_list[0], eq_list[-1])
                b_run = b_k + a_k * (edge * target)
                a_run = a_k * (1.0 - edge)
            else:
                b_run = a_k * b_run + b_k
                a_run = a_k * a_run
            sa_ref[j, k] = a_run
            sb_ref[j, k] = b_run

    def face_copy(c):
        return pltpu.make_async_remote_copy(
            src_ref=sb_ref.at[far0 + c, depth - 1],
            dst_ref=pb_ref.at[c],
            send_sem=face_ssem.at[c],
            recv_sem=face_rsem.at[c],
            device_id=(partner, v),
            device_id_type=MESH,
        )

    def far_block(c, carry):
        local_block(far0 + c)
        face_copy(c).start()
        return carry

    def own_block(c, carry):
        local_block(own0 + c)
        return carry

    lax.fori_loop(0, half_blocks, far_block, 0)
    lax.fori_loop(0, half_blocks, own_block, 0)

    rate_copy().wait()
    prate_ref[...] = jnp.broadcast_to(rate_recv[0:1, :], (LANE, cells)).T


    def first_weight(x1):
        sign = jnp.where(x1 > 0, 1.0, -1.0)
        return sign * jnp.where(q == 0, 1.0, -1.0) > 0

    def pair_block(c, carry):
        j = own0 + c
        x1, _, _ = block_tables(j)
        sigma = stream_x * jnp.abs(x1)
        opening = 1.0 + sigma
        other = None
        for x in range(depth):
            a = sigma / (opening + prate_ref[x * cells_x : (x + 1) * cells_x, :])
            other = a if other is None else other * a
        face_copy(c).wait_recv()
        a_own = sa_ref[j, depth - 1]
        b_own = sb_ref[j, depth - 1]
        b_other = pb_ref[c]
        first = first_weight(x1)
        pair_a[c, 0] = other
        pair_a[c, 1] = a_own * other
        pair_b[c] = jnp.where(first, other * b_own + b_other, a_own * b_other + b_own)
        return carry

    lax.fori_loop(0, half_blocks, pair_block, 0)

    def down_copy(c):
        return pltpu.make_async_remote_copy(
            src_ref=od_ref.at[c],
            dst_ref=ed_ref.at[c],
            send_sem=dn_ssem.at[c],
            recv_sem=dn_rsem.at[c],
            device_id=(s + 2, v),
            device_id_type=MESH,
        )

    def up_copy(c):
        return pltpu.make_async_remote_copy(
            src_ref=ou_ref.at[c],
            dst_ref=eu_ref.at[c],
            send_sem=up_ssem.at[c],
            recv_sem=up_rsem.at[c],
            device_id=(s - 2, v),
            device_id_type=MESH,
        )

    def return_copy(c):
        return pltpu.make_async_remote_copy(
            src_ref=enter_send.at[c],
            dst_ref=enter_recv.at[c],
            send_sem=ret_ssem.at[c],
            recv_sem=ret_rsem.at[c],
            device_id=(partner, v),
            device_id_type=MESH,
        )

    @pl.when(p == 0)
    def _():
        ed_ref[...] = jnp.zeros_like(ed_ref)

    @pl.when(p == pairs - 1)
    def _():
        eu_ref[...] = jnp.zeros_like(eu_ref)

    back = pairs - 1 - p
    latest = jnp.maximum(p, back)

    def chain_step(t, carry):
        c_dn = t - p
        c_up = t - back
        c_end = t - latest

        @pl.when((c_dn >= 0) & (c_dn < half_blocks))
        def _():
            @pl.when(p > 0)
            def _():
                down_copy(c_dn).wait_recv()

            @pl.when(p < pairs - 1)
            def _():
                od_ref[c_dn] = pair_a[c_dn, 1] * ed_ref[c_dn] + pair_b[c_dn]
                down_copy(c_dn).start()

        @pl.when((c_up >= 0) & (c_up < half_blocks))
        def _():
            @pl.when(p < pairs - 1)
            def _():
                up_copy(c_up).wait_recv()

            @pl.when(p > 0)
            def _():
                ou_ref[c_up] = pair_a[c_up, 1] * eu_ref[c_up] + pair_b[c_up]
                up_copy(c_up).start()

        @pl.when((c_end >= 0) & (c_end < half_blocks))
        def _():
            j = own0 + c_end
            x1, _, _ = block_tables(j)
            enter = jnp.where(x1 > 0, ed_ref[c_end], eu_ref[c_end])
            first = first_weight(x1)
            after_own = sa_ref[j, depth - 1] * enter + sb_ref[j, depth - 1]
            after_other = pair_a[c_end, 0] * enter + pb_ref[c_end]
            enter_send[c_end] = jnp.where(first, after_own, enter)
            return_copy(c_end).start()
            enter_own[c_end] = jnp.where(first, enter, after_other)

        return carry

    lax.fori_loop(0, half_blocks + pairs - 1, chain_step, 0)

    def finish(j, enter):
        x1, _, _ = block_tables(j)
        pos1 = x1 > 0
        done = [sa_ref[j, k] * enter + sb_ref[j, k] for k in range(depth)]
        for x in range(depth):
            value = jnp.where(pos1, done[x], done[depth - 1 - x])
            for z in range(planes):
                out_ref[pl.ds(frow(x, 0, j, z) - pad, rows, stride=stride), :] = value[
                    z * rows : (z + 1) * rows
                ]

    def finish_own(c, carry):
        finish(own0 + c, enter_own[c])
        return carry

    def finish_far(c, carry):
        return_copy(c).wait_recv()
        finish(far0 + c, enter_recv[c])
        return carry

    lax.fori_loop(0, half_blocks, finish_own, 0)
    lax.fori_loop(0, half_blocks, finish_far, 0)

    for d in range(1, nvel):
        wall_copy(d).wait_send()
        mom_copy(d).wait_send()

    def drain(c, carry):
        face_copy(c).wait_send()
        return_copy(c).wait_send()

        @pl.when(p < pairs - 1)
        def _():
            down_copy(c).wait_send()

        @pl.when(p > 0)
        def _():
            up_copy(c).wait_send()

        return carry

    lax.fori_loop(0, half_blocks, drain, 0)


def shards(nspace, nvel, distribution, wall_mask, grid_point, mirror_slot):
    depth, rows, planes, width = distribution.shape
    blocks = width // LANE
    half = blocks // 2
    dims = (depth, rows, planes, blocks, nspace, nvel)
    count = depth * rows * planes * blocks
    stride = blocks * planes
    side = planes * rows
    cells = depth * side
    walls = depth * 2 * planes
    flat = (
        distribution.reshape(depth, rows, planes, blocks, LANE)
        .transpose(0, 1, 3, 2, 4)
        .reshape(count, LANE)
    )
    vmem = pl.BlockSpec(memory_space=pltpu.VMEM)
    face = (half, side, LANE)
    out = pl.pallas_call(
        functools.partial(kernel, dims),
        out_shape=jax.ShapeDtypeStruct((count, LANE), F32),
        in_specs=[
            pl.BlockSpec(memory_space=pltpu.SMEM),
            vmem,
            vmem,
            pl.BlockSpec(memory_space=pl.ANY),
        ],
        out_specs=vmem,
        scratch_shapes=[
            pltpu.VMEM((count + 2 * stride, LANE), F32),
            pltpu.VMEM((nvel, blocks * walls, LANE), F32),
            pltpu.VMEM((nvel * blocks * walls, LANE), BF16),
            pltpu.VMEM((nvel * blocks * walls, LANE), BF16),
            pltpu.VMEM((blocks, walls, LANE), F32),
            pltpu.VMEM((cells, width), BF16),
            pltpu.VMEM((cells, width), BF16),
            pltpu.VMEM((LANE, width), BF16),
            pltpu.VMEM((blocks, LANE, 3 * LANE), BF16),
            pltpu.VMEM((nvel, MOM, cells), F32),
            pltpu.VMEM((LANE, cells), F32),
            pltpu.VMEM((cells, LANE), BF16),
            pltpu.VMEM((cells, LANE), F32),
            pltpu.VMEM((cells, LANE), F32),
            pltpu.VMEM((8, cells), F32),
            pltpu.VMEM((8, cells), F32),
            pltpu.VMEM((blocks, depth, side, LANE), F32),
            pltpu.VMEM((blocks, depth, side, LANE), F32),
            pltpu.VMEM(face, F32),
            pltpu.VMEM((half, 2, side, LANE), F32),
            pltpu.VMEM(face, F32),
            pltpu.VMEM(face, F32),
            pltpu.VMEM(face, F32),
            pltpu.VMEM(face, F32),
            pltpu.VMEM(face, F32),
            pltpu.VMEM(face, F32),
            pltpu.VMEM(face, F32),
            pltpu.VMEM(face, F32),
            pltpu.SemaphoreType.DMA,
            pltpu.SemaphoreType.DMA((nvel - 1,)),
            pltpu.SemaphoreType.DMA((nvel - 1,)),
            pltpu.SemaphoreType.DMA((nvel - 1,)),
            pltpu.SemaphoreType.DMA((nvel - 1,)),
            pltpu.SemaphoreType.DMA((2,)),
        ]
        + [pltpu.SemaphoreType.DMA((half,))] * 8,
        compiler_params=pltpu.CompilerParams(
            collective_id=0, has_side_effects=True, vmem_limit_bytes=40 * 1024 * 1024
        ),
    )(wall_mask, grid_point.reshape(blocks, LANE), mirror_slot.reshape(blocks, LANE), flat)
    return (
        out.reshape(depth, rows, blocks, planes, LANE)
        .transpose(0, 1, 3, 2, 4)
        .reshape(depth, rows, planes, width)
    )


def solution(mesh):
    placed = (P("space", None, None, "vel"), P("space", None, None), P("vel"), P("vel"))
    body = functools.partial(shards, mesh.shape["space"], mesh.shape["vel"])
    return jax.shard_map(
        body, mesh=mesh, in_specs=placed, out_specs=P("space", None, None, "vel"), check_vma=False
    )
```

```python
import functools
import math

import jax
import jax.numpy as jnp
from jax import lax
from jax.experimental import pallas as pl
from jax.experimental.pallas import tpu as pltpu
from jax.sharding import PartitionSpec as P

VS = 16
LANE = 128
FEAT = 8
MOM = 16
MESH = pl.DeviceIdType.MESH

stream_x = 40.0
stream_y = 0.15
stream_z = 0.05
relaxation_multiplier = 0.05
shear_power_index = 0.81
diffusivity_ratio = 2.0 / 3.0

F32 = jnp.float32
BF16 = jnp.bfloat16


def rounded(x):
    return x.astype(BF16).astype(F32)


def velocity_rows(points):
    spacing = 8.0 / VS
    half = (VS - 1) / 2.0
    bits = VS.bit_length() - 1
    first = lax.shift_right_logical(points, 2 * bits).astype(F32)
    second = (lax.shift_right_logical(points, bits) & (VS - 1)).astype(F32)
    third = (points & (VS - 1)).astype(F32)
    return [(v - half) * spacing for v in (first, second, third)]


def stacked(rows, height):
    index = lax.broadcasted_iota(jnp.int32, (height, LANE), 0)
    out = jnp.zeros((height, LANE), F32)
    for k, row in enumerate(rows):
        out = jnp.where(index == k, row, out)
    return out


def kernel(
    dims,
    wall_mask,
    grid_ref,
    mirror_ref,
    f_hbm,
    out_ref,
    f_ref,
    wall_ref,
    wsplit_ref,
    pick_ref,
    cell_ref,
    eq_ref,
    mirrored_ref,
    fhi_ref,
    flo_ref,
    tmom_ref,
    gmat_ref,
    mom_ref,
    coef_ref,
    lhs_ref,
    rate_ref,
    prate_ref,
    rate_send,
    rate_recv,
    sa_ref,
    sb_ref,
    pb_ref,
    pair_a,
    pair_b,
    ed_ref,
    eu_ref,
    od_ref,
    ou_ref,
    enter_own,
    enter_send,
    enter_recv,
    f_sem,
    wall_ssem,
    wall_rsem,
    mom_ssem,
    mom_rsem,
    rate_sem,
    face_ssem,
    face_rsem,
    dn_ssem,
    dn_rsem,
    up_ssem,
    up_rsem,
    ret_ssem,
    ret_rsem,
):
    depth, rows, planes, blocks, nspace, nvel = dims
    stride = blocks * planes
    cells_x = planes * rows
    cells = depth * cells_x
    walls = depth * 2 * planes
    half_blocks = blocks // 2
    pairs = nspace // 2
    weight = (8.0 / VS) ** 3

    s = lax.axis_index("space")
    v = lax.axis_index("vel")
    q = lax.rem(s, 2)
    p = lax.div(s, 2)
    partner = s + 1 - 2 * q
    own0 = q * half_blocks
    far0 = (1 - q) * half_blocks

    def frow(x, y, j, z):
        return (x * rows + y) * stride + j * planes + z

    load = pltpu.make_async_copy(f_hbm, f_ref, f_sem)
    load.start()

    barrier = pltpu.get_barrier_semaphore()
    for d in range(1, nvel):
        pl.semaphore_signal(
            barrier, inc=1, device_id=(s, lax.rem(v + d, nvel)), device_id_type=MESH
        )
    pl.semaphore_signal(barrier, inc=1, device_id=(partner, v), device_id_type=MESH)

    @pl.when(p > 0)
    def _():
        pl.semaphore_signal(barrier, inc=1, device_id=(s - 2, v), device_id_type=MESH)

    @pl.when(p < pairs - 1)
    def _():
        pl.semaphore_signal(barrier, inc=1, device_id=(s + 2, v), device_id_type=MESH)

    tmom_ref[...] = jnp.zeros_like(tmom_ref)
    gmat_ref[...] = jnp.zeros_like(gmat_ref)
    coef_ref[...] = jnp.zeros_like(coef_ref)
    for j in range(blocks):
        x1, x2, x3 = velocity_rows(grid_ref[j : j + 1, :])
        one = jnp.ones_like(x1)
        square = x1 * x1 + x2 * x2 + x3 * x3
        cubic = [x * square for x in (x1, x2, x3)]
        cubic_hi = [rounded(x) for x in cubic]
        cubic_lo = [x - h for x, h in zip(cubic, cubic_hi)]
        table = [one, x1, x2, x3, x1 * x1, x2 * x2, x3 * x3, x1 * x2, x1 * x3, x2 * x3]
        tmom_ref[0:MOM, j * LANE : (j + 1) * LANE] = stacked(
            table + cubic_hi + cubic_lo, MOM
        ).astype(BF16)
        feat = stacked(table[:7], FEAT)
        zero = jnp.zeros_like(feat)
        for g in range(3):
            column = [zero] * 9
            for part in range(3):
                column[3 * part + g] = feat
            column = column + [zero]
            gmat_ref[j, 0 : 10 * FEAT, g * LANE : (g + 1) * LANE] = jnp.concatenate(
                column, axis=0
            ).astype(BF16)

        slot = mirror_ref[j : j + 1, :]
        index = lax.broadcasted_iota(jnp.int32, (2 * LANE, LANE), 0) & (LANE - 1)
        pick_ref[j] = jnp.where(index == (slot & (LANE - 1)), 1.0, 0.0).astype(BF16)

    load.wait()

    for x in range(depth):
        for w in range(2):
            for z in range(planes):
                r = (x * 2 + w) * planes + z
                y = (rows - 1) * w
                wall_ref[v, pl.ds(r, blocks, stride=walls), :] = f_ref[
                    pl.ds(frow(x, y, 0, z), blocks, stride=planes), :
                ]

    greetings = nvel + (p > 0).astype(jnp.int32) + (p < pairs - 1).astype(jnp.int32)
    pl.semaphore_wait(barrier, greetings)

    sibling = v + 1 - 2 * lax.rem(v, 2)
    twins = nvel // 2

    def far(base, m):
        return lax.rem(base + 2 * m + nvel, nvel)

    def wall_copy(k, origin, target):
        return pltpu.make_async_remote_copy(
            src_ref=wall_ref.at[origin],
            dst_ref=wall_ref.at[origin],
            send_sem=wall_ssem.at[k],
            recv_sem=wall_rsem.at[k],
            device_id=(s, target),
            device_id_type=MESH,
        )

    def wall_far(m):
        return wall_copy(m, v, far(v, m))

    def wall_far_arrival(m):
        return wall_copy(m, far(v, -m), far(v, m))

    def wall_forward(m):
        return wall_copy(twins - 1 + m, far(v, -m), sibling)

    def wall_forward_arrival(m):
        return wall_copy(twins - 1 + m, far(sibling, -m), sibling)

    def mom_copy(k):
        target = far(v if k % 2 == 0 else sibling, k // 2)
        return pltpu.make_async_remote_copy(
            src_ref=mom_ref.at[0],
            dst_ref=mom_ref.at[k],
            send_sem=mom_ssem.at[k - 1],
            recv_sem=mom_rsem.at[k - 1],
            device_id=(s, target),
            device_id_type=MESH,
        )

    for m in range(1, twins):
        wall_far(m).start()
    wall_copy(0, v, sibling).start()

    for x in range(depth):
        for z in range(planes):
            base = (x * planes + z) * rows
            for j in range(blocks):
                part = f_ref[pl.ds(frow(x, 0, j, z), rows, stride=stride), :]
                hi = part.astype(BF16)
                lo = (part - hi.astype(F32)).astype(BF16)
                cell_ref[j, x, z * rows : (z + 1) * rows, :] = part
                fhi_ref[base : base + rows, j * LANE : (j + 1) * LANE] = hi
                flo_ref[base : base + rows, j * LANE : (j + 1) * LANE] = lo
    contract = (((1,), (1,)), ((), ()))
    sums = lax.dot_general(
        fhi_ref[...], tmom_ref[...], contract, preferred_element_type=F32
    ) + lax.dot_general(flo_ref[...], tmom_ref[...], contract, preferred_element_type=F32)
    mom_ref[0] = sums.T[0:MOM, :]
    for d in range(nvel - 1, 0, -1):
        mom_copy(d).start()
    for m in range(1, twins):
        wall_far_arrival(m).wait_recv()
        wall_forward(m).start()
    total = mom_ref[0]
    for d in range(1, nvel):
        mom_copy(d).wait_recv()
        total = total + mom_ref[d]
    total = total * weight

    raw = [total[k : k + 1, :] for k in range(MOM)]
    density = raw[0]
    momentum = raw[1:4]
    flow = [m / density for m in momentum]
    tensor = [[raw[4], raw[7], raw[8]], [raw[7], raw[5], raw[9]], [raw[8], raw[9], raw[6]]]
    third = [raw[10 + k] + raw[13 + k] for k in range(3)]
    trace = raw[4] + raw[5] + raw[6]
    flow_sq = flow[0] * flow[0] + flow[1] * flow[1] + flow[2] * flow[2]
    temperature = (trace - density * flow_sq) / (3.0 * density)
    flow_mom = flow[0] * momentum[0] + flow[1] * momentum[1] + flow[2] * momentum[2]
    heat = []
    for k in range(3):
        contracted = flow[0] * tensor[k][0] + flow[1] * tensor[k][1] + flow[2] * tensor[k][2]
        heat.append(
            0.5
            * (
                third[k]
                - 2.0 * contracted
                + flow_sq * momentum[k]
                - flow[k] * trace
                + 2.0 * flow[k] * flow_mom
                - flow[k] * flow_sq * density
            )
        )
    log_t = jnp.log(temperature)
    inverse_t = 1.0 / temperature
    rate = relaxation_multiplier * density * jnp.exp((1.0 - shear_power_index) * log_t)

    rate_send[...] = jnp.broadcast_to(rate, rate_send.shape)

    def rate_copy():
        return pltpu.make_async_remote_copy(
            src_ref=rate_send,
            dst_ref=rate_recv,
            send_sem=rate_sem.at[0],
            recv_sem=rate_sem.at[1],
            device_id=(partner, v),
            device_id_type=MESH,
        )

    rate_copy().start()
    scale = (1.0 - diffusivity_ratio) / 5.0 * inverse_t * inverse_t / density
    flow_heat = flow[0] * heat[0] + flow[1] * heat[1] + flow[2] * heat[2]
    exponent = [
        jnp.log(density) - 1.5 * (log_t + math.log(2.0 * math.pi)) - 0.5 * flow_sq * inverse_t
    ]
    exponent += [u * inverse_t for u in flow] + [-0.5 * inverse_t] * 3
    linear = [-scale * flow_heat] + [scale * h for h in heat]
    bracket = [flow_sq * inverse_t - 5.0]
    bracket += [-2.0 * u * inverse_t for u in flow] + [inverse_t] * 3
    for g, group in enumerate((exponent, linear, bracket)):
        for k, row in enumerate(group):
            coef_ref[g * FEAT + k : g * FEAT + k + 1, :] = row
    whole = coef_ref[0 : 3 * FEAT, :]
    hi = rounded(whole)
    mid = rounded(whole - hi)
    coef_ref[0 : 3 * FEAT, :] = hi
    coef_ref[3 * FEAT : 6 * FEAT, :] = mid
    coef_ref[6 * FEAT : 9 * FEAT, :] = whole - hi - mid
    lhs_ref[...] = coef_ref[...].T.astype(BF16)
    rate_ref[...] = jnp.broadcast_to(rate, (LANE, cells)).T

    for j in range(blocks):
        got = jnp.dot(lhs_ref[...], gmat_ref[j], preferred_element_type=F32)
        eq_ref[j] = jnp.exp(got[:, :LANE]) * (
            1.0 + got[:, LANE : 2 * LANE] * got[:, 2 * LANE :]
        )

    wall_copy(0, sibling, sibling).wait_recv()
    for m in range(1, twins):
        wall_forward_arrival(m).wait_recv()
    everywhere = wall_ref[...].reshape(nvel * blocks * walls, LANE)
    whi = everywhere.astype(BF16)
    wsplit_ref[:, :LANE] = whi
    wsplit_ref[:, LANE:] = (everywhere - whi.astype(F32)).astype(BF16)
    for j in range(blocks):
        high = lax.shift_right_logical(mirror_ref[j : j + 1, :], LANE.bit_length() - 1)
        found = jnp.dot(wsplit_ref[...], pick_ref[j], preferred_element_type=F32)
        acc = jnp.zeros((walls, LANE), F32)
        for h in range(nvel * blocks):
            acc = acc + jnp.where(high == h, found[h * walls : (h + 1) * walls], 0.0)
        mirrored_ref[j] = acc

    first_edge = jnp.where(s == 0, 1.0, 0.0).astype(F32)
    last_edge = jnp.where(s == nspace - 1, 1.0, 0.0).astype(F32)
    row_index = lax.broadcasted_iota(jnp.int32, (rows, LANE), 0)

    def block_tables(j):
        return velocity_rows(grid_ref[pl.ds(j, 1), :])

    def local_block(j):
        x1, x2, x3 = block_tables(j)
        pos1 = x1 > 0
        pos2 = x2 > 0
        pos3 = x3 > 0
        coef_y = stream_y * jnp.abs(x2)
        coef_z = stream_z * jnp.abs(x3)
        coef_f = 1.0 - coef_y - coef_z
        sigma = stream_x * jnp.abs(x1)
        opening = 1.0 + sigma
        edge = jnp.where(pos1, first_edge, last_edge)
        mirrored = mirrored_ref[j]
        a_list, b_list, eq_list = [], [], []
        for x in range(depth):
            base = x * cells_x
            equilibrium = eq_ref[j, base : base + cells_x, :]
            rates = rate_ref[base : base + cells_x, :]
            inverse = 1.0 / (opening + rates)
            source = rates * equilibrium
            values = [
                cell_ref[j, x, z * rows : (z + 1) * rows, :] for z in range(planes)
            ]
            parts = []
            for z in range(planes):
                low = (x * 2) * planes + z
                high = (x * 2 + 1) * planes + z
                mask_low = jnp.full((1, LANE), wall_mask[x, 0, z])
                mask_high = jnp.full((1, LANE), wall_mask[x, 1, z])
                eq_z = equilibrium[z * rows : (z + 1) * rows]
                ghost_low = jnp.where(mask_low == 1, mirrored[low : low + 1], eq_z[0:1])
                ghost_high = jnp.where(
                    mask_high == 1, mirrored[high : high + 1], eq_z[rows - 1 : rows]
                )
                below = pltpu.roll(values[z], 1, axis=0)
                above = pltpu.roll(values[z], rows - 1, axis=0)
                below = jnp.where(row_index == 0, ghost_low, below)
                above = jnp.where(row_index == rows - 1, ghost_high, above)
                side = jnp.where(pos2, below, above)
                before, after = values[(z - 1) % planes], values[(z + 1) % planes]
                if (z - 1) % planes == (z + 1) % planes:
                    plane = before
                else:
                    plane = jnp.where(pos3, before, after)
                parts.append(coef_f * values[z] + coef_y * side + coef_z * plane)
            b_list.append((jnp.concatenate(parts, axis=0) + source) * inverse)
            a_list.append(sigma * inverse)
            if x in (0, depth - 1):
                eq_list.append(equilibrium)
        a_run = b_run = None
        for k in range(depth):
            a_k = jnp.where(pos1, a_list[k], a_list[depth - 1 - k])
            b_k = jnp.where(pos1, b_list[k], b_list[depth - 1 - k])
            if k == 0:
                target = jnp.where(pos1, eq_list[0], eq_list[-1])
                b_run = b_k + a_k * (edge * target)
                a_run = a_k * (1.0 - edge)
            else:
                b_run = a_k * b_run + b_k
                a_run = a_k * a_run
            sa_ref[j, k] = a_run
            sb_ref[j, k] = b_run

    def face_copy(c):
        return pltpu.make_async_remote_copy(
            src_ref=sb_ref.at[far0 + c, depth - 1],
            dst_ref=pb_ref.at[c],
            send_sem=face_ssem.at[c],
            recv_sem=face_rsem.at[c],
            device_id=(partner, v),
            device_id_type=MESH,
        )

    def far_block(c, carry):
        local_block(far0 + c)
        face_copy(c).start()
        return carry

    def own_block(c, carry):
        local_block(own0 + c)
        return carry

    lax.fori_loop(0, half_blocks, far_block, 0)
    lax.fori_loop(0, half_blocks, own_block, 0)

    rate_copy().wait()
    prate_ref[...] = jnp.broadcast_to(rate_recv[0:1, :], (LANE, cells)).T


    def first_weight(x1):
        sign = jnp.where(x1 > 0, 1.0, -1.0)
        return sign * jnp.where(q == 0, 1.0, -1.0) > 0

    def pair_block(c, carry):
        j = own0 + c
        x1, _, _ = block_tables(j)
        sigma = stream_x * jnp.abs(x1)
        opening = 1.0 + sigma
        other = None
        for x in range(depth):
            a = sigma / (opening + prate_ref[x * cells_x : (x + 1) * cells_x, :])
            other = a if other is None else other * a
        face_copy(c).wait_recv()
        a_own = sa_ref[j, depth - 1]
        b_own = sb_ref[j, depth - 1]
        b_other = pb_ref[c]
        first = first_weight(x1)
        pair_a[c, 0] = other
        pair_a[c, 1] = a_own * other
        pair_b[c] = jnp.where(first, other * b_own + b_other, a_own * b_other + b_own)
        return carry

    lax.fori_loop(0, half_blocks, pair_block, 0)

    def down_copy(c):
        return pltpu.make_async_remote_copy(
            src_ref=od_ref.at[c],
            dst_ref=ed_ref.at[c],
            send_sem=dn_ssem.at[c],
            recv_sem=dn_rsem.at[c],
            device_id=(s + 2, v),
            device_id_type=MESH,
        )

    def up_copy(c):
        return pltpu.make_async_remote_copy(
            src_ref=ou_ref.at[c],
            dst_ref=eu_ref.at[c],
            send_sem=up_ssem.at[c],
            recv_sem=up_rsem.at[c],
            device_id=(s - 2, v),
            device_id_type=MESH,
        )

    def return_copy(c):
        return pltpu.make_async_remote_copy(
            src_ref=enter_send.at[c],
            dst_ref=enter_recv.at[c],
            send_sem=ret_ssem.at[c],
            recv_sem=ret_rsem.at[c],
            device_id=(partner, v),
            device_id_type=MESH,
        )

    @pl.when(p == 0)
    def _():
        ed_ref[...] = jnp.zeros_like(ed_ref)

    @pl.when(p == pairs - 1)
    def _():
        eu_ref[...] = jnp.zeros_like(eu_ref)

    back = pairs - 1 - p
    latest = jnp.maximum(p, back)

    def chain_step(t, carry):
        c_dn = t - p
        c_up = t - back
        c_end = t - latest

        @pl.when((c_dn >= 0) & (c_dn < half_blocks))
        def _():
            @pl.when(p > 0)
            def _():
                down_copy(c_dn).wait_recv()

            @pl.when(p < pairs - 1)
            def _():
                od_ref[c_dn] = pair_a[c_dn, 1] * ed_ref[c_dn] + pair_b[c_dn]
                down_copy(c_dn).start()

        @pl.when((c_up >= 0) & (c_up < half_blocks))
        def _():
            @pl.when(p < pairs - 1)
            def _():
                up_copy(c_up).wait_recv()

            @pl.when(p > 0)
            def _():
                ou_ref[c_up] = pair_a[c_up, 1] * eu_ref[c_up] + pair_b[c_up]
                up_copy(c_up).start()

        @pl.when((c_end >= 0) & (c_end < half_blocks))
        def _():
            j = own0 + c_end
            x1, _, _ = block_tables(j)
            enter = jnp.where(x1 > 0, ed_ref[c_end], eu_ref[c_end])
            first = first_weight(x1)
            after_own = sa_ref[j, depth - 1] * enter + sb_ref[j, depth - 1]
            after_other = pair_a[c_end, 0] * enter + pb_ref[c_end]
            enter_send[c_end] = jnp.where(first, after_own, enter)
            return_copy(c_end).start()
            enter_own[c_end] = jnp.where(first, enter, after_other)

        return carry

    lax.fori_loop(0, half_blocks + pairs - 1, chain_step, 0)

    def finish(j, enter):
        x1, _, _ = block_tables(j)
        pos1 = x1 > 0
        done = [sa_ref[j, k] * enter + sb_ref[j, k] for k in range(depth)]
        for x in range(depth):
            value = jnp.where(pos1, done[x], done[depth - 1 - x])
            for z in range(planes):
                out_ref[pl.ds(frow(x, 0, j, z), rows, stride=stride), :] = value[
                    z * rows : (z + 1) * rows
                ]

    def finish_own(c, carry):
        finish(own0 + c, enter_own[c])
        return carry

    def finish_far(c, carry):
        return_copy(c).wait_recv()
        finish(far0 + c, enter_recv[c])
        return carry

    lax.fori_loop(0, half_blocks, finish_own, 0)
    lax.fori_loop(0, half_blocks, finish_far, 0)

    wall_copy(0, v, sibling).wait_send()
    for m in range(1, twins):
        wall_far(m).wait_send()
        wall_forward(m).wait_send()
    for d in range(1, nvel):
        mom_copy(d).wait_send()

    def drain(c, carry):
        face_copy(c).wait_send()
        return_copy(c).wait_send()

        @pl.when(p < pairs - 1)
        def _():
            down_copy(c).wait_send()

        @pl.when(p > 0)
        def _():
            up_copy(c).wait_send()

        return carry

    lax.fori_loop(0, half_blocks, drain, 0)


def shards(nspace, nvel, distribution, wall_mask, grid_point, mirror_slot):
    depth, rows, planes, width = distribution.shape
    blocks = width // LANE
    half = blocks // 2
    dims = (depth, rows, planes, blocks, nspace, nvel)
    count = depth * rows * planes * blocks
    stride = blocks * planes
    side = planes * rows
    cells = depth * side
    walls = depth * 2 * planes
    flat = (
        distribution.reshape(depth, rows, planes, blocks, LANE)
        .transpose(0, 1, 3, 2, 4)
        .reshape(count, LANE)
    )
    vmem = pl.BlockSpec(memory_space=pltpu.VMEM)
    face = (half, side, LANE)
    out = pl.pallas_call(
        functools.partial(kernel, dims),
        out_shape=jax.ShapeDtypeStruct((count, LANE), F32),
        in_specs=[
            pl.BlockSpec(memory_space=pltpu.SMEM),
            vmem,
            vmem,
            pl.BlockSpec(memory_space=pl.ANY),
        ],
        out_specs=vmem,
        scratch_shapes=[
            pltpu.VMEM((count, LANE), F32),
            pltpu.VMEM((nvel, blocks * walls, LANE), F32),
            pltpu.VMEM((nvel * blocks * walls, 2 * LANE), BF16),
            pltpu.VMEM((blocks, 2 * LANE, LANE), BF16),
            pltpu.VMEM((blocks, depth, side, LANE), F32),
            pltpu.VMEM((blocks, cells, LANE), F32),
            pltpu.VMEM((blocks, walls, LANE), F32),
            pltpu.VMEM((cells, width), BF16),
            pltpu.VMEM((cells, width), BF16),
            pltpu.VMEM((LANE, width), BF16),
            pltpu.VMEM((blocks, LANE, 3 * LANE), BF16),
            pltpu.VMEM((nvel, MOM, cells), F32),
            pltpu.VMEM((LANE, cells), F32),
            pltpu.VMEM((cells, LANE), BF16),
            pltpu.VMEM((cells, LANE), F32),
            pltpu.VMEM((cells, LANE), F32),
            pltpu.VMEM((8, cells), F32),
            pltpu.VMEM((8, cells), F32),
            pltpu.VMEM((blocks, depth, side, LANE), F32),
            pltpu.VMEM((blocks, depth, side, LANE), F32),
            pltpu.VMEM(face, F32),
            pltpu.VMEM((half, 2, side, LANE), F32),
            pltpu.VMEM(face, F32),
            pltpu.VMEM(face, F32),
            pltpu.VMEM(face, F32),
            pltpu.VMEM(face, F32),
            pltpu.VMEM(face, F32),
            pltpu.VMEM(face, F32),
            pltpu.VMEM(face, F32),
            pltpu.VMEM(face, F32),
            pltpu.SemaphoreType.DMA,
            pltpu.SemaphoreType.DMA((nvel - 1,)),
            pltpu.SemaphoreType.DMA((nvel - 1,)),
            pltpu.SemaphoreType.DMA((nvel - 1,)),
            pltpu.SemaphoreType.DMA((nvel - 1,)),
            pltpu.SemaphoreType.DMA((2,)),
        ]
        + [pltpu.SemaphoreType.DMA((half,))] * 8,
        compiler_params=pltpu.CompilerParams(
            collective_id=0, has_side_effects=True, vmem_limit_bytes=40 * 1024 * 1024
        ),
    )(wall_mask, grid_point.reshape(blocks, LANE), mirror_slot.reshape(blocks, LANE), flat)
    return (
        out.reshape(depth, rows, blocks, planes, LANE)
        .transpose(0, 1, 3, 2, 4)
        .reshape(depth, rows, planes, width)
    )


def solution(mesh):
    placed = (P("space", None, None, "vel"), P("space", None, None), P("vel"), P("vel"))
    body = functools.partial(shards, mesh.shape["space"], mesh.shape["vel"])
    return jax.shard_map(
        body, mesh=mesh, in_specs=placed, out_specs=P("space", None, None, "vel"), check_vma=False
    )
```

```python
import functools
import math

import jax
import jax.numpy as jnp
from jax import lax
from jax.experimental import pallas as pl
from jax.experimental.pallas import tpu as pltpu
from jax.sharding import PartitionSpec as P

VS = 16
LANE = 128
FEAT = 8
MOM = 16
MESH = pl.DeviceIdType.MESH

stream_x = 40.0
stream_y = 0.15
stream_z = 0.05
relaxation_multiplier = 0.05
shear_power_index = 0.81
diffusivity_ratio = 2.0 / 3.0

F32 = jnp.float32
BF16 = jnp.bfloat16


def rounded(x):
    return x.astype(BF16).astype(F32)


def velocity_rows(points):
    spacing = 8.0 / VS
    half = (VS - 1) / 2.0
    bits = VS.bit_length() - 1
    first = lax.shift_right_logical(points, 2 * bits).astype(F32)
    second = (lax.shift_right_logical(points, bits) & (VS - 1)).astype(F32)
    third = (points & (VS - 1)).astype(F32)
    return [(v - half) * spacing for v in (first, second, third)]


def stacked(rows, height):
    index = lax.broadcasted_iota(jnp.int32, (height, LANE), 0)
    out = jnp.zeros((height, LANE), F32)
    for k, row in enumerate(rows):
        out = jnp.where(index == k, row, out)
    return out


def kernel(
    dims,
    wall_mask,
    grid_ref,
    mirror_ref,
    f_hbm,
    out_ref,
    f_ref,
    wall_ref,
    wsplit_ref,
    pick_ref,
    cell_ref,
    eq_ref,
    mirrored_ref,
    fhi_ref,
    flo_ref,
    tmom_ref,
    gmat_ref,
    mom_ref,
    coef_ref,
    lhs_ref,
    rate_ref,
    prate_ref,
    rate_send,
    rate_recv,
    sa_ref,
    sb_ref,
    pb_ref,
    pair_a,
    pair_b,
    ed_ref,
    eu_ref,
    od_ref,
    ou_ref,
    enter_own,
    enter_send,
    enter_recv,
    f_sem,
    wall_ssem,
    wall_rsem,
    mom_ssem,
    mom_rsem,
    rate_sem,
    face_ssem,
    face_rsem,
    dn_ssem,
    dn_rsem,
    up_ssem,
    up_rsem,
    ret_ssem,
    ret_rsem,
):
    depth, rows, planes, blocks, nspace, nvel = dims
    stride = blocks * planes
    cells_x = planes * rows
    cells = depth * cells_x
    walls = depth * 2 * planes
    half_blocks = blocks // 2
    pairs = nspace // 2
    weight = (8.0 / VS) ** 3

    s = lax.axis_index("space")
    v = lax.axis_index("vel")
    q = lax.rem(s, 2)
    p = lax.div(s, 2)
    partner = s + 1 - 2 * q
    own0 = q * half_blocks
    far0 = (1 - q) * half_blocks

    def frow(x, y, j, z):
        return (x * rows + y) * stride + j * planes + z

    load = pltpu.make_async_copy(f_hbm, f_ref, f_sem)
    load.start()

    barrier = pltpu.get_barrier_semaphore()
    for d in range(1, nvel):
        pl.semaphore_signal(
            barrier, inc=1, device_id=(s, lax.rem(v + d, nvel)), device_id_type=MESH
        )
    pl.semaphore_signal(barrier, inc=1, device_id=(partner, v), device_id_type=MESH)

    @pl.when(p > 0)
    def _():
        pl.semaphore_signal(barrier, inc=1, device_id=(s - 2, v), device_id_type=MESH)

    @pl.when(p < pairs - 1)
    def _():
        pl.semaphore_signal(barrier, inc=1, device_id=(s + 2, v), device_id_type=MESH)

    tmom_ref[...] = jnp.zeros_like(tmom_ref)
    gmat_ref[...] = jnp.zeros_like(gmat_ref)
    coef_ref[...] = jnp.zeros_like(coef_ref)
    for j in range(blocks):
        x1, x2, x3 = velocity_rows(grid_ref[j : j + 1, :])
        one = jnp.ones_like(x1)
        square = x1 * x1 + x2 * x2 + x3 * x3
        cubic = [x * square for x in (x1, x2, x3)]
        cubic_hi = [rounded(x) for x in cubic]
        cubic_lo = [x - h for x, h in zip(cubic, cubic_hi)]
        table = [one, x1, x2, x3, x1 * x1, x2 * x2, x3 * x3, x1 * x2, x1 * x3, x2 * x3]
        tmom_ref[0:MOM, j * LANE : (j + 1) * LANE] = stacked(
            table + cubic_hi + cubic_lo, MOM
        ).astype(BF16)
        feat = stacked(table[:7], FEAT)
        zero = jnp.zeros_like(feat)
        for g in range(3):
            column = [zero] * 9
            for part in range(3):
                column[3 * part + g] = feat
            column = column + [zero]
            gmat_ref[j, 0 : 10 * FEAT, g * LANE : (g + 1) * LANE] = jnp.concatenate(
                column, axis=0
            ).astype(BF16)

        slot = mirror_ref[j : j + 1, :]
        index = lax.broadcasted_iota(jnp.int32, (2 * LANE, LANE), 0) & (LANE - 1)
        pick_ref[j] = jnp.where(index == (slot & (LANE - 1)), 1.0, 0.0).astype(BF16)

    load.wait()

    for x in range(depth):
        for w in range(2):
            for z in range(planes):
                r = (x * 2 + w) * planes + z
                y = (rows - 1) * w
                wall_ref[v, pl.ds(r, blocks, stride=walls), :] = f_ref[
                    pl.ds(frow(x, y, 0, z), blocks, stride=planes), :
                ]

    greetings = nvel + (p > 0).astype(jnp.int32) + (p < pairs - 1).astype(jnp.int32)
    pl.semaphore_wait(barrier, greetings)

    sibling = v + 1 - 2 * lax.rem(v, 2)
    twins = nvel // 2

    def far(base, m):
        return lax.rem(base + 2 * m + nvel, nvel)

    def wall_copy(k, origin, target):
        return pltpu.make_async_remote_copy(
            src_ref=wall_ref.at[origin],
            dst_ref=wall_ref.at[origin],
            send_sem=wall_ssem.at[k],
            recv_sem=wall_rsem.at[k],
            device_id=(s, target),
            device_id_type=MESH,
        )

    def wall_far(m):
        return wall_copy(m, v, far(v, m))

    def wall_far_arrival(m):
        return wall_copy(m, far(v, -m), far(v, m))

    def wall_forward(m):
        return wall_copy(twins - 1 + m, far(v, -m), sibling)

    def wall_forward_arrival(m):
        return wall_copy(twins - 1 + m, far(sibling, -m), sibling)

    def mom_copy(k):
        target = far(v if k % 2 == 0 else sibling, k // 2)
        return pltpu.make_async_remote_copy(
            src_ref=mom_ref.at[0],
            dst_ref=mom_ref.at[k],
            send_sem=mom_ssem.at[k - 1],
            recv_sem=mom_rsem.at[k - 1],
            device_id=(s, target),
            device_id_type=MESH,
        )

    for m in range(1, twins):
        wall_far(m).start()
    wall_copy(0, v, sibling).start()

    for x in range(depth):
        for z in range(planes):
            base = (x * planes + z) * rows
            for j in range(blocks):
                part = f_ref[pl.ds(frow(x, 0, j, z), rows, stride=stride), :]
                hi = part.astype(BF16)
                lo = (part - hi.astype(F32)).astype(BF16)
                cell_ref[j, x, z * rows : (z + 1) * rows, :] = part
                fhi_ref[base : base + rows, j * LANE : (j + 1) * LANE] = hi
                flo_ref[base : base + rows, j * LANE : (j + 1) * LANE] = lo
    contract = (((1,), (1,)), ((), ()))
    sums = lax.dot_general(
        fhi_ref[...], tmom_ref[...], contract, preferred_element_type=F32
    ) + lax.dot_general(flo_ref[...], tmom_ref[...], contract, preferred_element_type=F32)
    mom_ref[0] = sums.T[0:MOM, :]
    for d in range(nvel - 1, 0, -1):
        mom_copy(d).start()
    for m in range(1, twins):
        wall_far_arrival(m).wait_recv()
        wall_forward(m).start()
    row_index = lax.broadcasted_iota(jnp.int32, (rows, LANE), 0)

    def block_tables(j):
        return velocity_rows(grid_ref[pl.ds(j, 1), :])

    def flux_block(j, carry):
        _, x2, x3 = block_tables(j)
        pos2 = x2 > 0
        pos3 = x3 > 0
        coef_y = stream_y * jnp.abs(x2)
        coef_z = stream_z * jnp.abs(x3)
        coef_f = 1.0 - coef_y - coef_z
        for x in range(depth):
            values = [
                cell_ref[j, x, z * rows : (z + 1) * rows, :] for z in range(planes)
            ]
            for z in range(planes):
                below = jnp.where(row_index == 0, 0.0, pltpu.roll(values[z], 1, axis=0))
                above = jnp.where(
                    row_index == rows - 1, 0.0, pltpu.roll(values[z], rows - 1, axis=0)
                )
                side = jnp.where(pos2, below, above)
                before, after = values[(z - 1) % planes], values[(z + 1) % planes]
                if (z - 1) % planes == (z + 1) % planes:
                    plane = before
                else:
                    plane = jnp.where(pos3, before, after)
                sb_ref[j, x, z * rows : (z + 1) * rows, :] = (
                    coef_f * values[z] + coef_y * side + coef_z * plane
                )
        return carry

    lax.fori_loop(0, blocks, flux_block, 0)

    total = mom_ref[0]
    for d in range(1, nvel):
        mom_copy(d).wait_recv()
        total = total + mom_ref[d]
    total = total * weight

    raw = [total[k : k + 1, :] for k in range(MOM)]
    density = raw[0]
    momentum = raw[1:4]
    flow = [m / density for m in momentum]
    tensor = [[raw[4], raw[7], raw[8]], [raw[7], raw[5], raw[9]], [raw[8], raw[9], raw[6]]]
    third = [raw[10 + k] + raw[13 + k] for k in range(3)]
    trace = raw[4] + raw[5] + raw[6]
    flow_sq = flow[0] * flow[0] + flow[1] * flow[1] + flow[2] * flow[2]
    temperature = (trace - density * flow_sq) / (3.0 * density)
    flow_mom = flow[0] * momentum[0] + flow[1] * momentum[1] + flow[2] * momentum[2]
    heat = []
    for k in range(3):
        contracted = flow[0] * tensor[k][0] + flow[1] * tensor[k][1] + flow[2] * tensor[k][2]
        heat.append(
            0.5
            * (
                third[k]
                - 2.0 * contracted
                + flow_sq * momentum[k]
                - flow[k] * trace
                + 2.0 * flow[k] * flow_mom
                - flow[k] * flow_sq * density
            )
        )
    log_t = jnp.log(temperature)
    inverse_t = 1.0 / temperature
    rate = relaxation_multiplier * density * jnp.exp((1.0 - shear_power_index) * log_t)

    rate_send[...] = jnp.broadcast_to(rate, rate_send.shape)

    def rate_copy():
        return pltpu.make_async_remote_copy(
            src_ref=rate_send,
            dst_ref=rate_recv,
            send_sem=rate_sem.at[0],
            recv_sem=rate_sem.at[1],
            device_id=(partner, v),
            device_id_type=MESH,
        )

    rate_copy().start()
    scale = (1.0 - diffusivity_ratio) / 5.0 * inverse_t * inverse_t / density
    flow_heat = flow[0] * heat[0] + flow[1] * heat[1] + flow[2] * heat[2]
    exponent = [
        jnp.log(density) - 1.5 * (log_t + math.log(2.0 * math.pi)) - 0.5 * flow_sq * inverse_t
    ]
    exponent += [u * inverse_t for u in flow] + [-0.5 * inverse_t] * 3
    linear = [-scale * flow_heat] + [scale * h for h in heat]
    bracket = [flow_sq * inverse_t - 5.0]
    bracket += [-2.0 * u * inverse_t for u in flow] + [inverse_t] * 3
    for g, group in enumerate((exponent, linear, bracket)):
        for k, row in enumerate(group):
            coef_ref[g * FEAT + k : g * FEAT + k + 1, :] = row
    whole = coef_ref[0 : 3 * FEAT, :]
    hi = rounded(whole)
    mid = rounded(whole - hi)
    coef_ref[0 : 3 * FEAT, :] = hi
    coef_ref[3 * FEAT : 6 * FEAT, :] = mid
    coef_ref[6 * FEAT : 9 * FEAT, :] = whole - hi - mid
    lhs_ref[...] = coef_ref[...].T.astype(BF16)
    rate_ref[...] = jnp.broadcast_to(rate, (LANE, cells)).T

    for j in range(blocks):
        got = jnp.dot(lhs_ref[...], gmat_ref[j], preferred_element_type=F32)
        eq_ref[j] = jnp.exp(got[:, :LANE]) * (
            1.0 + got[:, LANE : 2 * LANE] * got[:, 2 * LANE :]
        )

    wall_copy(0, sibling, sibling).wait_recv()
    for m in range(1, twins):
        wall_forward_arrival(m).wait_recv()
    everywhere = wall_ref[...].reshape(nvel * blocks * walls, LANE)
    whi = everywhere.astype(BF16)
    wsplit_ref[:, :LANE] = whi
    wsplit_ref[:, LANE:] = (everywhere - whi.astype(F32)).astype(BF16)
    for j in range(blocks):
        high = lax.shift_right_logical(mirror_ref[j : j + 1, :], LANE.bit_length() - 1)
        found = jnp.dot(wsplit_ref[...], pick_ref[j], preferred_element_type=F32)
        acc = jnp.zeros((walls, LANE), F32)
        for h in range(nvel * blocks):
            acc = acc + jnp.where(high == h, found[h * walls : (h + 1) * walls], 0.0)
        mirrored_ref[j] = acc

    first_edge = jnp.where(s == 0, 1.0, 0.0).astype(F32)
    last_edge = jnp.where(s == nspace - 1, 1.0, 0.0).astype(F32)
    def local_block(j):
        x1, x2, _ = block_tables(j)
        pos1 = x1 > 0
        pos2 = x2 > 0
        coef_y = stream_y * jnp.abs(x2)
        coef_low = jnp.where(pos2, coef_y, 0.0)
        coef_high = jnp.where(pos2, 0.0, coef_y)
        sigma = stream_x * jnp.abs(x1)
        opening = 1.0 + sigma
        edge = jnp.where(pos1, first_edge, last_edge)
        mirrored = mirrored_ref[j]
        group_index = lax.broadcasted_iota(jnp.int32, (8, LANE), 0)
        a_list, b_list, eq_list = [], [], []
        for x in range(depth):
            base = x * cells_x
            equilibrium = eq_ref[j, base : base + cells_x, :]
            rates = rate_ref[base : base + cells_x, :]
            inverse = 1.0 / (opening + rates)
            parts = []
            for z in range(planes):
                low = (x * 2) * planes + z
                high = (x * 2 + 1) * planes + z
                mask_low = jnp.full((1, LANE), wall_mask[0, z, x])
                mask_high = jnp.full((1, LANE), wall_mask[1, z, x])
                eq_z = equilibrium[z * rows : (z + 1) * rows]
                ghost_low = jnp.where(mask_low == 1, mirrored[low : low + 1], eq_z[0:1])
                ghost_high = jnp.where(
                    mask_high == 1, mirrored[high : high + 1], eq_z[rows - 1 : rows]
                )
                flux = sb_ref[j, x, z * rows : (z + 1) * rows, :]
                parts += [
                    flux[:8] + jnp.where(group_index == 0, coef_low * ghost_low, 0.0),
                    flux[8 : rows - 8],
                    flux[rows - 8 :] + jnp.where(group_index == 7, coef_high * ghost_high, 0.0),
                ]
            b_list.append((jnp.concatenate(parts, axis=0) + rates * equilibrium) * inverse)
            a_list.append(sigma * inverse)
            if x in (0, depth - 1):
                eq_list.append(equilibrium)
        a_run = b_run = None
        for k in range(depth):
            a_k = jnp.where(pos1, a_list[k], a_list[depth - 1 - k])
            b_k = jnp.where(pos1, b_list[k], b_list[depth - 1 - k])
            if k == 0:
                target = jnp.where(pos1, eq_list[0], eq_list[-1])
                b_run = b_k + a_k * (edge * target)
                a_run = a_k * (1.0 - edge)
            else:
                b_run = a_k * b_run + b_k
                a_run = a_k * a_run
            sa_ref[j, k] = a_run
            sb_ref[j, k] = b_run

    def face_copy(c):
        return pltpu.make_async_remote_copy(
            src_ref=sb_ref.at[far0 + c, depth - 1],
            dst_ref=pb_ref.at[c],
            send_sem=face_ssem.at[c],
            recv_sem=face_rsem.at[c],
            device_id=(partner, v),
            device_id_type=MESH,
        )

    def far_block(c, carry):
        local_block(far0 + c)
        face_copy(c).start()
        return carry

    lax.fori_loop(0, half_blocks, far_block, 0)

    rate_copy().wait()
    prate_ref[...] = jnp.broadcast_to(rate_recv[0:1, :], (LANE, cells)).T


    def first_weight(x1):
        sign = jnp.where(x1 > 0, 1.0, -1.0)
        return sign * jnp.where(q == 0, 1.0, -1.0) > 0

    def pair_block(c):
        j = own0 + c
        local_block(j)
        x1, _, _ = block_tables(j)
        sigma = stream_x * jnp.abs(x1)
        opening = 1.0 + sigma
        other = None
        for x in range(depth):
            a = sigma / (opening + prate_ref[x * cells_x : (x + 1) * cells_x, :])
            other = a if other is None else other * a
        face_copy(c).wait_recv()
        a_own = sa_ref[j, depth - 1]
        b_own = sb_ref[j, depth - 1]
        b_other = pb_ref[c]
        first = first_weight(x1)
        pair_a[c, 0] = other
        pair_a[c, 1] = a_own * other
        pair_b[c] = jnp.where(first, other * b_own + b_other, a_own * b_other + b_own)

    def down_copy(c):
        return pltpu.make_async_remote_copy(
            src_ref=od_ref.at[c],
            dst_ref=ed_ref.at[c],
            send_sem=dn_ssem.at[c],
            recv_sem=dn_rsem.at[c],
            device_id=(s + 2, v),
            device_id_type=MESH,
        )

    def up_copy(c):
        return pltpu.make_async_remote_copy(
            src_ref=ou_ref.at[c],
            dst_ref=eu_ref.at[c],
            send_sem=up_ssem.at[c],
            recv_sem=up_rsem.at[c],
            device_id=(s - 2, v),
            device_id_type=MESH,
        )

    def return_copy(c):
        return pltpu.make_async_remote_copy(
            src_ref=enter_send.at[c],
            dst_ref=enter_recv.at[c],
            send_sem=ret_ssem.at[c],
            recv_sem=ret_rsem.at[c],
            device_id=(partner, v),
            device_id_type=MESH,
        )

    @pl.when(p == 0)
    def _():
        ed_ref[...] = jnp.zeros_like(ed_ref)

    @pl.when(p == pairs - 1)
    def _():
        eu_ref[...] = jnp.zeros_like(eu_ref)

    back = pairs - 1 - p
    latest = jnp.maximum(p, back)

    def chain_step(t, carry):
        c_dn = t - p
        c_up = t - back
        c_end = t - latest

        @pl.when(t < half_blocks)
        def _():
            pair_block(t)

        @pl.when((c_dn >= 0) & (c_dn < half_blocks))
        def _():
            @pl.when(p > 0)
            def _():
                down_copy(c_dn).wait_recv()

            @pl.when(p < pairs - 1)
            def _():
                od_ref[c_dn] = pair_a[c_dn, 1] * ed_ref[c_dn] + pair_b[c_dn]
                down_copy(c_dn).start()

        @pl.when((c_up >= 0) & (c_up < half_blocks))
        def _():
            @pl.when(p < pairs - 1)
            def _():
                up_copy(c_up).wait_recv()

            @pl.when(p > 0)
            def _():
                ou_ref[c_up] = pair_a[c_up, 1] * eu_ref[c_up] + pair_b[c_up]
                up_copy(c_up).start()

        @pl.when((c_end >= 0) & (c_end < half_blocks))
        def _():
            j = own0 + c_end
            x1, _, _ = block_tables(j)
            enter = jnp.where(x1 > 0, ed_ref[c_end], eu_ref[c_end])
            first = first_weight(x1)
            after_own = sa_ref[j, depth - 1] * enter + sb_ref[j, depth - 1]
            after_other = pair_a[c_end, 0] * enter + pb_ref[c_end]
            enter_send[c_end] = jnp.where(first, after_own, enter)
            return_copy(c_end).start()
            enter_own[c_end] = jnp.where(first, enter, after_other)

        return carry

    lax.fori_loop(0, half_blocks + pairs - 1, chain_step, 0)

    def finish(j, enter):
        x1, _, _ = block_tables(j)
        pos1 = x1 > 0
        done = [sa_ref[j, k] * enter + sb_ref[j, k] for k in range(depth)]
        for x in range(depth):
            value = jnp.where(pos1, done[x], done[depth - 1 - x])
            for z in range(planes):
                out_ref[pl.ds(frow(x, 0, j, z), rows, stride=stride), :] = value[
                    z * rows : (z + 1) * rows
                ]

    def finish_own(c, carry):
        finish(own0 + c, enter_own[c])
        return carry

    def finish_far(c, carry):
        return_copy(c).wait_recv()
        finish(far0 + c, enter_recv[c])
        return carry

    lax.fori_loop(0, half_blocks, finish_own, 0)
    lax.fori_loop(0, half_blocks, finish_far, 0)

    wall_copy(0, v, sibling).wait_send()
    for m in range(1, twins):
        wall_far(m).wait_send()
        wall_forward(m).wait_send()
    for d in range(1, nvel):
        mom_copy(d).wait_send()

    def drain(c, carry):
        face_copy(c).wait_send()
        return_copy(c).wait_send()

        @pl.when(p < pairs - 1)
        def _():
            down_copy(c).wait_send()

        @pl.when(p > 0)
        def _():
            up_copy(c).wait_send()

        return carry

    lax.fori_loop(0, half_blocks, drain, 0)


def shards(nspace, nvel, distribution, wall_mask, grid_point, mirror_slot):
    depth, rows, planes, width = distribution.shape
    blocks = width // LANE
    half = blocks // 2
    dims = (depth, rows, planes, blocks, nspace, nvel)
    count = depth * rows * planes * blocks
    stride = blocks * planes
    side = planes * rows
    cells = depth * side
    walls = depth * 2 * planes
    flat = (
        distribution.reshape(depth, rows, planes, blocks, LANE)
        .transpose(0, 1, 3, 2, 4)
        .reshape(count, LANE)
    )
    vmem = pl.BlockSpec(memory_space=pltpu.VMEM)
    face = (half, side, LANE)
    out = pl.pallas_call(
        functools.partial(kernel, dims),
        out_shape=jax.ShapeDtypeStruct((count, LANE), F32),
        in_specs=[
            pl.BlockSpec(memory_space=pltpu.SMEM),
            vmem,
            vmem,
            pl.BlockSpec(memory_space=pl.ANY),
        ],
        out_specs=vmem,
        scratch_shapes=[
            pltpu.VMEM((count, LANE), F32),
            pltpu.VMEM((nvel, blocks * walls, LANE), F32),
            pltpu.VMEM((nvel * blocks * walls, 2 * LANE), BF16),
            pltpu.VMEM((blocks, 2 * LANE, LANE), BF16),
            pltpu.VMEM((blocks, depth, side, LANE), F32),
            pltpu.VMEM((blocks, cells, LANE), F32),
            pltpu.VMEM((blocks, walls, LANE), F32),
            pltpu.VMEM((cells, width), BF16),
            pltpu.VMEM((cells, width), BF16),
            pltpu.VMEM((LANE, width), BF16),
            pltpu.VMEM((blocks, LANE, 3 * LANE), BF16),
            pltpu.VMEM((nvel, MOM, cells), F32),
            pltpu.VMEM((LANE, cells), F32),
            pltpu.VMEM((cells, LANE), BF16),
            pltpu.VMEM((cells, LANE), F32),
            pltpu.VMEM((cells, LANE), F32),
            pltpu.VMEM((8, cells), F32),
            pltpu.VMEM((8, cells), F32),
            pltpu.VMEM((blocks, depth, side, LANE), F32),
            pltpu.VMEM((blocks, depth, side, LANE), F32),
            pltpu.VMEM(face, F32),
            pltpu.VMEM((half, 2, side, LANE), F32),
            pltpu.VMEM(face, F32),
            pltpu.VMEM(face, F32),
            pltpu.VMEM(face, F32),
            pltpu.VMEM(face, F32),
            pltpu.VMEM(face, F32),
            pltpu.VMEM(face, F32),
            pltpu.VMEM(face, F32),
            pltpu.VMEM(face, F32),
            pltpu.SemaphoreType.DMA,
            pltpu.SemaphoreType.DMA((nvel - 1,)),
            pltpu.SemaphoreType.DMA((nvel - 1,)),
            pltpu.SemaphoreType.DMA((nvel - 1,)),
            pltpu.SemaphoreType.DMA((nvel - 1,)),
            pltpu.SemaphoreType.DMA((2,)),
        ]
        + [pltpu.SemaphoreType.DMA((half,))] * 8,
        compiler_params=pltpu.CompilerParams(
            collective_id=0, has_side_effects=True, vmem_limit_bytes=62 * 1024 * 1024
        ),
    )(wall_mask.transpose(1, 2, 0), grid_point.reshape(blocks, LANE), mirror_slot.reshape(blocks, LANE), flat)
    return (
        out.reshape(depth, rows, blocks, planes, LANE)
        .transpose(0, 1, 3, 2, 4)
        .reshape(depth, rows, planes, width)
    )


def solution(mesh):
    placed = (P("space", None, None, "vel"), P("space", None, None), P("vel"), P("vel"))
    body = functools.partial(shards, mesh.shape["space"], mesh.shape["vel"])
    return jax.shard_map(
        body, mesh=mesh, in_specs=placed, out_specs=P("space", None, None, "vel"), check_vma=False
    )
```

```python
import functools
import math

import jax
import jax.numpy as jnp
from jax import lax
from jax.experimental import pallas as pl
from jax.experimental.pallas import tpu as pltpu
from jax.sharding import PartitionSpec as P

VS = 16
LANE = 128
FEAT = 8
MOM = 16
MESH = pl.DeviceIdType.MESH

stream_x = 40.0
stream_y = 0.15
stream_z = 0.05
relaxation_multiplier = 0.05
shear_power_index = 0.81
diffusivity_ratio = 2.0 / 3.0

F32 = jnp.float32
BF16 = jnp.bfloat16


def rounded(x):
    return x.astype(BF16).astype(F32)


def velocity_rows(points):
    spacing = 8.0 / VS
    half = (VS - 1) / 2.0
    bits = VS.bit_length() - 1
    first = lax.shift_right_logical(points, 2 * bits).astype(F32)
    second = (lax.shift_right_logical(points, bits) & (VS - 1)).astype(F32)
    third = (points & (VS - 1)).astype(F32)
    return [(v - half) * spacing for v in (first, second, third)]


def stacked(rows, height):
    index = lax.broadcasted_iota(jnp.int32, (height, LANE), 0)
    out = jnp.zeros((height, LANE), F32)
    for k, row in enumerate(rows):
        out = jnp.where(index == k, row, out)
    return out


def kernel(
    dims,
    wall_mask,
    grid_ref,
    mirror_ref,
    f_ref,
    out_ref,
    wall_ref,
    wsplit_ref,
    pick_ref,
    cell_ref,
    eq_ref,
    mirrored_ref,
    fhi_ref,
    flo_ref,
    tmom_ref,
    gmat_ref,
    mom_ref,
    coef_ref,
    lhs_ref,
    rate_ref,
    prate_ref,
    rate_send,
    rate_recv,
    sa_ref,
    sb_ref,
    pb_ref,
    pair_a,
    pair_b,
    ed_ref,
    eu_ref,
    od_ref,
    ou_ref,
    enter_own,
    enter_send,
    enter_recv,
    wall_ssem,
    wall_rsem,
    mom_ssem,
    mom_rsem,
    rate_sem,
    face_ssem,
    face_rsem,
    dn_ssem,
    dn_rsem,
    up_ssem,
    up_rsem,
    ret_ssem,
    ret_rsem,
):
    depth, rows, planes, blocks, nspace, nvel = dims
    stride = blocks * planes
    cells_x = planes * rows
    cells = depth * cells_x
    walls = depth * 2 * planes
    half_blocks = blocks // 2
    pairs = nspace // 2
    weight = (8.0 / VS) ** 3

    s = lax.axis_index("space")
    v = lax.axis_index("vel")
    q = lax.rem(s, 2)
    p = lax.div(s, 2)
    partner = s + 1 - 2 * q
    own0 = q * half_blocks
    far0 = (1 - q) * half_blocks

    def frow(x, y, j, z):
        return (x * rows + y) * stride + j * planes + z

    barrier = pltpu.get_barrier_semaphore()
    for d in range(1, nvel):
        pl.semaphore_signal(
            barrier, inc=1, device_id=(s, lax.rem(v + d, nvel)), device_id_type=MESH
        )
    pl.semaphore_signal(barrier, inc=1, device_id=(partner, v), device_id_type=MESH)

    @pl.when(p > 0)
    def _():
        pl.semaphore_signal(barrier, inc=1, device_id=(s - 2, v), device_id_type=MESH)

    @pl.when(p < pairs - 1)
    def _():
        pl.semaphore_signal(barrier, inc=1, device_id=(s + 2, v), device_id_type=MESH)

    tmom_ref[...] = jnp.zeros_like(tmom_ref)
    gmat_ref[...] = jnp.zeros_like(gmat_ref)
    coef_ref[...] = jnp.zeros_like(coef_ref)
    for j in range(blocks):
        x1, x2, x3 = velocity_rows(grid_ref[j : j + 1, :])
        one = jnp.ones_like(x1)
        square = x1 * x1 + x2 * x2 + x3 * x3
        cubic = [x * square for x in (x1, x2, x3)]
        cubic_hi = [rounded(x) for x in cubic]
        cubic_lo = [x - h for x, h in zip(cubic, cubic_hi)]
        table = [one, x1, x2, x3, x1 * x1, x2 * x2, x3 * x3, x1 * x2, x1 * x3, x2 * x3]
        tmom_ref[0:MOM, j * LANE : (j + 1) * LANE] = stacked(
            table + cubic_hi + cubic_lo, MOM
        ).astype(BF16)
        feat = stacked(table[:7], FEAT)
        zero = jnp.zeros_like(feat)
        for g in range(3):
            column = [zero] * 9
            for part in range(3):
                column[3 * part + g] = feat
            column = column + [zero]
            gmat_ref[j, 0 : 10 * FEAT, g * LANE : (g + 1) * LANE] = jnp.concatenate(
                column, axis=0
            ).astype(BF16)

        slot = mirror_ref[j : j + 1, :]
        index = lax.broadcasted_iota(jnp.int32, (2 * LANE, LANE), 0) & (LANE - 1)
        pick_ref[j] = jnp.where(index == (slot & (LANE - 1)), 1.0, 0.0).astype(BF16)

    for x in range(depth):
        for w in range(2):
            for z in range(planes):
                r = (x * 2 + w) * planes + z
                y = (rows - 1) * w
                wall_ref[v, pl.ds(r, blocks, stride=walls), :] = f_ref[
                    pl.ds(frow(x, y, 0, z), blocks, stride=planes), :
                ]

    for x in range(depth):
        for z in range(planes):
            base = (x * planes + z) * rows
            for j in range(blocks):
                part = f_ref[pl.ds(frow(x, 0, j, z), rows, stride=stride), :]
                hi = part.astype(BF16)
                lo = (part - hi.astype(F32)).astype(BF16)
                cell_ref[j, x, z * rows : (z + 1) * rows, :] = part
                fhi_ref[base : base + rows, j * LANE : (j + 1) * LANE] = hi
                flo_ref[base : base + rows, j * LANE : (j + 1) * LANE] = lo

    greetings = nvel + (p > 0).astype(jnp.int32) + (p < pairs - 1).astype(jnp.int32)
    pl.semaphore_wait(barrier, greetings)

    sibling = v + 1 - 2 * lax.rem(v, 2)
    twins = nvel // 2

    def far(base, m):
        return lax.rem(base + 2 * m + nvel, nvel)

    def wall_copy(k, origin, target):
        return pltpu.make_async_remote_copy(
            src_ref=wall_ref.at[origin],
            dst_ref=wall_ref.at[origin],
            send_sem=wall_ssem.at[k],
            recv_sem=wall_rsem.at[k],
            device_id=(s, target),
            device_id_type=MESH,
        )

    def wall_far(m):
        return wall_copy(m, v, far(v, m))

    def wall_far_arrival(m):
        return wall_copy(m, far(v, -m), far(v, m))

    def wall_forward(m):
        return wall_copy(twins - 1 + m, far(v, -m), sibling)

    def wall_forward_arrival(m):
        return wall_copy(twins - 1 + m, far(sibling, -m), sibling)

    def mom_copy(k):
        target = far(v if k % 2 == 0 else sibling, k // 2)
        return pltpu.make_async_remote_copy(
            src_ref=mom_ref.at[0],
            dst_ref=mom_ref.at[k],
            send_sem=mom_ssem.at[k - 1],
            recv_sem=mom_rsem.at[k - 1],
            device_id=(s, target),
            device_id_type=MESH,
        )

    for m in range(1, twins):
        wall_far(m).start()
    wall_copy(0, v, sibling).start()

    contract = (((1,), (1,)), ((), ()))
    sums = lax.dot_general(
        fhi_ref[...], tmom_ref[...], contract, preferred_element_type=F32
    ) + lax.dot_general(flo_ref[...], tmom_ref[...], contract, preferred_element_type=F32)
    mom_ref[0] = sums.T[0:MOM, :]
    for d in range(nvel - 1, 0, -1):
        mom_copy(d).start()
    for m in range(1, twins):
        wall_far_arrival(m).wait_recv()
        wall_forward(m).start()
    row_index = lax.broadcasted_iota(jnp.int32, (rows, LANE), 0)

    def block_tables(j):
        return velocity_rows(grid_ref[pl.ds(j, 1), :])

    def flux_block(j, carry):
        _, x2, x3 = block_tables(j)
        pos2 = x2 > 0
        pos3 = x3 > 0
        coef_y = stream_y * jnp.abs(x2)
        coef_z = stream_z * jnp.abs(x3)
        coef_f = 1.0 - coef_y - coef_z
        for x in range(depth):
            values = [
                cell_ref[j, x, z * rows : (z + 1) * rows, :] for z in range(planes)
            ]
            for z in range(planes):
                below = jnp.where(row_index == 0, 0.0, pltpu.roll(values[z], 1, axis=0))
                above = jnp.where(
                    row_index == rows - 1, 0.0, pltpu.roll(values[z], rows - 1, axis=0)
                )
                side = jnp.where(pos2, below, above)
                before, after = values[(z - 1) % planes], values[(z + 1) % planes]
                if (z - 1) % planes == (z + 1) % planes:
                    plane = before
                else:
                    plane = jnp.where(pos3, before, after)
                sb_ref[j, x, z * rows : (z + 1) * rows, :] = (
                    coef_f * values[z] + coef_y * side + coef_z * plane
                )
        return carry

    lax.fori_loop(0, blocks, flux_block, 0)

    total = mom_ref[0]
    for d in range(1, nvel):
        mom_copy(d).wait_recv()
        total = total + mom_ref[d]
    total = total * weight

    raw = [total[k : k + 1, :] for k in range(MOM)]
    density = raw[0]
    momentum = raw[1:4]
    flow = [m / density for m in momentum]
    tensor = [[raw[4], raw[7], raw[8]], [raw[7], raw[5], raw[9]], [raw[8], raw[9], raw[6]]]
    third = [raw[10 + k] + raw[13 + k] for k in range(3)]
    trace = raw[4] + raw[5] + raw[6]
    flow_sq = flow[0] * flow[0] + flow[1] * flow[1] + flow[2] * flow[2]
    temperature = (trace - density * flow_sq) / (3.0 * density)
    flow_mom = flow[0] * momentum[0] + flow[1] * momentum[1] + flow[2] * momentum[2]
    heat = []
    for k in range(3):
        contracted = flow[0] * tensor[k][0] + flow[1] * tensor[k][1] + flow[2] * tensor[k][2]
        heat.append(
            0.5
            * (
                third[k]
                - 2.0 * contracted
                + flow_sq * momentum[k]
                - flow[k] * trace
                + 2.0 * flow[k] * flow_mom
                - flow[k] * flow_sq * density
            )
        )
    log_t = jnp.log(temperature)
    inverse_t = 1.0 / temperature
    rate = relaxation_multiplier * density * jnp.exp((1.0 - shear_power_index) * log_t)

    rate_send[...] = jnp.broadcast_to(rate, rate_send.shape)

    def rate_copy():
        return pltpu.make_async_remote_copy(
            src_ref=rate_send,
            dst_ref=rate_recv,
            send_sem=rate_sem.at[0],
            recv_sem=rate_sem.at[1],
            device_id=(partner, v),
            device_id_type=MESH,
        )

    rate_copy().start()
    scale = (1.0 - diffusivity_ratio) / 5.0 * inverse_t * inverse_t / density
    flow_heat = flow[0] * heat[0] + flow[1] * heat[1] + flow[2] * heat[2]
    exponent = [
        jnp.log(density) - 1.5 * (log_t + math.log(2.0 * math.pi)) - 0.5 * flow_sq * inverse_t
    ]
    exponent += [u * inverse_t for u in flow] + [-0.5 * inverse_t] * 3
    linear = [-scale * flow_heat] + [scale * h for h in heat]
    bracket = [flow_sq * inverse_t - 5.0]
    bracket += [-2.0 * u * inverse_t for u in flow] + [inverse_t] * 3
    for g, group in enumerate((exponent, linear, bracket)):
        for k, row in enumerate(group):
            coef_ref[g * FEAT + k : g * FEAT + k + 1, :] = row
    whole = coef_ref[0 : 3 * FEAT, :]
    hi = rounded(whole)
    mid = rounded(whole - hi)
    coef_ref[0 : 3 * FEAT, :] = hi
    coef_ref[3 * FEAT : 6 * FEAT, :] = mid
    coef_ref[6 * FEAT : 9 * FEAT, :] = whole - hi - mid
    lhs_ref[...] = coef_ref[...].T.astype(BF16)
    rate_ref[...] = jnp.broadcast_to(rate, (LANE, cells)).T

    for j in range(blocks):
        got = jnp.dot(lhs_ref[...], gmat_ref[j], preferred_element_type=F32)
        eq_ref[j] = jnp.exp(got[:, :LANE]) * (
            1.0 + got[:, LANE : 2 * LANE] * got[:, 2 * LANE :]
        )

    wall_copy(0, sibling, sibling).wait_recv()
    for m in range(1, twins):
        wall_forward_arrival(m).wait_recv()
    everywhere = wall_ref[...].reshape(nvel * blocks * walls, LANE)
    whi = everywhere.astype(BF16)
    wsplit_ref[:, :LANE] = whi
    wsplit_ref[:, LANE:] = (everywhere - whi.astype(F32)).astype(BF16)
    for j in range(blocks):
        high = lax.shift_right_logical(mirror_ref[j : j + 1, :], LANE.bit_length() - 1)
        found = jnp.dot(wsplit_ref[...], pick_ref[j], preferred_element_type=F32)
        acc = jnp.zeros((walls, LANE), F32)
        for h in range(nvel * blocks):
            acc = acc + jnp.where(high == h, found[h * walls : (h + 1) * walls], 0.0)
        mirrored_ref[j] = acc

    first_edge = jnp.where(s == 0, 1.0, 0.0).astype(F32)
    last_edge = jnp.where(s == nspace - 1, 1.0, 0.0).astype(F32)
    def local_block(j):
        x1, x2, _ = block_tables(j)
        pos1 = x1 > 0
        pos2 = x2 > 0
        coef_y = stream_y * jnp.abs(x2)
        coef_low = jnp.where(pos2, coef_y, 0.0)
        coef_high = jnp.where(pos2, 0.0, coef_y)
        sigma = stream_x * jnp.abs(x1)
        opening = 1.0 + sigma
        edge = jnp.where(pos1, first_edge, last_edge)
        mirrored = mirrored_ref[j]
        group_index = lax.broadcasted_iota(jnp.int32, (8, LANE), 0)
        a_list, b_list, eq_list = [], [], []
        for x in range(depth):
            base = x * cells_x
            equilibrium = eq_ref[j, base : base + cells_x, :]
            rates = rate_ref[base : base + cells_x, :]
            inverse = 1.0 / (opening + rates)
            parts = []
            for z in range(planes):
                low = (x * 2) * planes + z
                high = (x * 2 + 1) * planes + z
                mask_low = jnp.full((1, LANE), wall_mask[0, z, x])
                mask_high = jnp.full((1, LANE), wall_mask[1, z, x])
                eq_z = equilibrium[z * rows : (z + 1) * rows]
                ghost_low = jnp.where(mask_low == 1, mirrored[low : low + 1], eq_z[0:1])
                ghost_high = jnp.where(
                    mask_high == 1, mirrored[high : high + 1], eq_z[rows - 1 : rows]
                )
                flux = sb_ref[j, x, z * rows : (z + 1) * rows, :]
                parts += [
                    flux[:8] + jnp.where(group_index == 0, coef_low * ghost_low, 0.0),
                    flux[8 : rows - 8],
                    flux[rows - 8 :] + jnp.where(group_index == 7, coef_high * ghost_high, 0.0),
                ]
            b_list.append((jnp.concatenate(parts, axis=0) + rates * equilibrium) * inverse)
            a_list.append(sigma * inverse)
            if x in (0, depth - 1):
                eq_list.append(equilibrium)
        a_run = b_run = None
        for k in range(depth):
            a_k = jnp.where(pos1, a_list[k], a_list[depth - 1 - k])
            b_k = jnp.where(pos1, b_list[k], b_list[depth - 1 - k])
            if k == 0:
                target = jnp.where(pos1, eq_list[0], eq_list[-1])
                b_run = b_k + a_k * (edge * target)
                a_run = a_k * (1.0 - edge)
            else:
                b_run = a_k * b_run + b_k
                a_run = a_k * a_run
            sa_ref[j, k] = a_run
            sb_ref[j, k] = b_run

    def band(z):
        return pl.ds(z * rows, rows)

    def face_copy(c, z):
        return pltpu.make_async_remote_copy(
            src_ref=sb_ref.at[far0 + c, depth - 1, band(z)],
            dst_ref=pb_ref.at[c, band(z)],
            send_sem=face_ssem.at[c, z],
            recv_sem=face_rsem.at[c, z],
            device_id=(partner, v),
            device_id_type=MESH,
        )

    def far_block(c, carry):
        local_block(far0 + c)
        for z in range(planes):
            face_copy(c, z).start()
        return carry

    lax.fori_loop(0, half_blocks, far_block, 0)

    rate_copy().wait()
    prate_ref[...] = jnp.broadcast_to(rate_recv[0:1, :], (LANE, cells)).T


    def first_weight(x1):
        sign = jnp.where(x1 > 0, 1.0, -1.0)
        return sign * jnp.where(q == 0, 1.0, -1.0) > 0

    def pair_block(c):
        j = own0 + c
        local_block(j)
        x1, _, _ = block_tables(j)
        sigma = stream_x * jnp.abs(x1)
        opening = 1.0 + sigma
        other = None
        for x in range(depth):
            a = sigma / (opening + prate_ref[x * cells_x : (x + 1) * cells_x, :])
            other = a if other is None else other * a
        for z in range(planes):
            face_copy(c, z).wait_recv()
        a_own = sa_ref[j, depth - 1]
        b_own = sb_ref[j, depth - 1]
        b_other = pb_ref[c]
        first = first_weight(x1)
        pair_a[c, 0] = other
        pair_a[c, 1] = a_own * other
        pair_b[c] = jnp.where(first, other * b_own + b_other, a_own * b_other + b_own)

    def down_copy(c, z):
        return pltpu.make_async_remote_copy(
            src_ref=od_ref.at[c, band(z)],
            dst_ref=ed_ref.at[c, band(z)],
            send_sem=dn_ssem.at[c, z],
            recv_sem=dn_rsem.at[c, z],
            device_id=(s + 2, v),
            device_id_type=MESH,
        )

    def up_copy(c, z):
        return pltpu.make_async_remote_copy(
            src_ref=ou_ref.at[c, band(z)],
            dst_ref=eu_ref.at[c, band(z)],
            send_sem=up_ssem.at[c, z],
            recv_sem=up_rsem.at[c, z],
            device_id=(s - 2, v),
            device_id_type=MESH,
        )

    def return_copy(c, z):
        return pltpu.make_async_remote_copy(
            src_ref=enter_send.at[c, band(z)],
            dst_ref=enter_recv.at[c, band(z)],
            send_sem=ret_ssem.at[c, z],
            recv_sem=ret_rsem.at[c, z],
            device_id=(partner, v),
            device_id_type=MESH,
        )

    @pl.when(p == 0)
    def _():
        ed_ref[...] = jnp.zeros_like(ed_ref)

    @pl.when(p == pairs - 1)
    def _():
        eu_ref[...] = jnp.zeros_like(eu_ref)

    back = pairs - 1 - p
    latest = jnp.maximum(p, back)

    def chain_step(t, carry):
        c_dn = t - p
        c_up = t - back
        c_end = t - latest

        @pl.when(t < half_blocks)
        def _():
            pair_block(t)

        @pl.when((c_dn >= 0) & (c_dn < half_blocks))
        def _():
            for z in range(planes):
                at = (c_dn, band(z))

                @pl.when(p > 0)
                def _():
                    down_copy(c_dn, z).wait_recv()

                @pl.when(p < pairs - 1)
                def _():
                    od_ref[at] = pair_a[c_dn, 1, band(z)] * ed_ref[at] + pair_b[at]
                    down_copy(c_dn, z).start()

        @pl.when((c_up >= 0) & (c_up < half_blocks))
        def _():
            for z in range(planes):
                at = (c_up, band(z))

                @pl.when(p < pairs - 1)
                def _():
                    up_copy(c_up, z).wait_recv()

                @pl.when(p > 0)
                def _():
                    ou_ref[at] = pair_a[c_up, 1, band(z)] * eu_ref[at] + pair_b[at]
                    up_copy(c_up, z).start()

        @pl.when((c_end >= 0) & (c_end < half_blocks))
        def _():
            j = own0 + c_end
            x1, _, _ = block_tables(j)
            first = first_weight(x1)
            for z in range(planes):
                at = (c_end, band(z))
                enter = jnp.where(x1 > 0, ed_ref[at], eu_ref[at])
                last = (j, depth - 1, band(z))
                after_own = sa_ref[last] * enter + sb_ref[last]
                after_other = pair_a[c_end, 0, band(z)] * enter + pb_ref[at]
                enter_send[at] = jnp.where(first, after_own, enter)
                return_copy(c_end, z).start()
                enter_own[at] = jnp.where(first, enter, after_other)

        return carry

    lax.fori_loop(0, half_blocks + pairs - 1, chain_step, 0)

    def finish(j, enter):
        x1, _, _ = block_tables(j)
        pos1 = x1 > 0
        done = [sa_ref[j, k] * enter + sb_ref[j, k] for k in range(depth)]
        for x in range(depth):
            value = jnp.where(pos1, done[x], done[depth - 1 - x])
            for z in range(planes):
                out_ref[pl.ds(frow(x, 0, j, z), rows, stride=stride), :] = value[
                    z * rows : (z + 1) * rows
                ]

    def finish_own(c, carry):
        finish(own0 + c, enter_own[c])
        return carry

    def finish_far(c, carry):
        for z in range(planes):
            return_copy(c, z).wait_recv()
        finish(far0 + c, enter_recv[c])
        return carry

    lax.fori_loop(0, half_blocks, finish_own, 0)
    lax.fori_loop(0, half_blocks, finish_far, 0)

    wall_copy(0, v, sibling).wait_send()
    for m in range(1, twins):
        wall_far(m).wait_send()
        wall_forward(m).wait_send()
    for d in range(1, nvel):
        mom_copy(d).wait_send()

    def drain(c, carry):
        for z in range(planes):
            face_copy(c, z).wait_send()
            return_copy(c, z).wait_send()

            @pl.when(p < pairs - 1)
            def _():
                down_copy(c, z).wait_send()

            @pl.when(p > 0)
            def _():
                up_copy(c, z).wait_send()

        return carry

    lax.fori_loop(0, half_blocks, drain, 0)


def shards(nspace, nvel, distribution, wall_mask, grid_point, mirror_slot):
    depth, rows, planes, width = distribution.shape
    blocks = width // LANE
    half = blocks // 2
    dims = (depth, rows, planes, blocks, nspace, nvel)
    count = depth * rows * planes * blocks
    stride = blocks * planes
    side = planes * rows
    cells = depth * side
    walls = depth * 2 * planes
    flat = (
        distribution.reshape(depth, rows, planes, blocks, LANE)
        .transpose(0, 1, 3, 2, 4)
        .reshape(count, LANE)
    )
    vmem = pl.BlockSpec(memory_space=pltpu.VMEM)
    face = (half, side, LANE)
    out = pl.pallas_call(
        functools.partial(kernel, dims),
        out_shape=jax.ShapeDtypeStruct((count, LANE), F32),
        in_specs=[
            pl.BlockSpec(memory_space=pltpu.SMEM),
            vmem,
            vmem,
            vmem,
        ],
        out_specs=vmem,
        scratch_shapes=[
            pltpu.VMEM((nvel, blocks * walls, LANE), F32),
            pltpu.VMEM((nvel * blocks * walls, 2 * LANE), BF16),
            pltpu.VMEM((blocks, 2 * LANE, LANE), BF16),
            pltpu.VMEM((blocks, depth, side, LANE), F32),
            pltpu.VMEM((blocks, cells, LANE), F32),
            pltpu.VMEM((blocks, walls, LANE), F32),
            pltpu.VMEM((cells, width), BF16),
            pltpu.VMEM((cells, width), BF16),
            pltpu.VMEM((LANE, width), BF16),
            pltpu.VMEM((blocks, LANE, 3 * LANE), BF16),
            pltpu.VMEM((nvel, MOM, cells), F32),
            pltpu.VMEM((LANE, cells), F32),
            pltpu.VMEM((cells, LANE), BF16),
            pltpu.VMEM((cells, LANE), F32),
            pltpu.VMEM((cells, LANE), F32),
            pltpu.VMEM((8, cells), F32),
            pltpu.VMEM((8, cells), F32),
            pltpu.VMEM((blocks, depth, side, LANE), F32),
            pltpu.VMEM((blocks, depth, side, LANE), F32),
            pltpu.VMEM(face, F32),
            pltpu.VMEM((half, 2, side, LANE), F32),
            pltpu.VMEM(face, F32),
            pltpu.VMEM(face, F32),
            pltpu.VMEM(face, F32),
            pltpu.VMEM(face, F32),
            pltpu.VMEM(face, F32),
            pltpu.VMEM(face, F32),
            pltpu.VMEM(face, F32),
            pltpu.VMEM(face, F32),
            pltpu.SemaphoreType.DMA((nvel - 1,)),
            pltpu.SemaphoreType.DMA((nvel - 1,)),
            pltpu.SemaphoreType.DMA((nvel - 1,)),
            pltpu.SemaphoreType.DMA((nvel - 1,)),
            pltpu.SemaphoreType.DMA((2,)),
        ]
        + [pltpu.SemaphoreType.DMA((half, planes))] * 8,
        compiler_params=pltpu.CompilerParams(
            collective_id=0, has_side_effects=True, vmem_limit_bytes=40 * 1024 * 1024
        ),
    )(wall_mask.transpose(1, 2, 0), grid_point.reshape(blocks, LANE), mirror_slot.reshape(blocks, LANE), flat)
    return (
        out.reshape(depth, rows, blocks, planes, LANE)
        .transpose(0, 1, 3, 2, 4)
        .reshape(depth, rows, planes, width)
    )


def solution(mesh):
    placed = (P("space", None, None, "vel"), P("space", None, None), P("vel"), P("vel"))
    body = functools.partial(shards, mesh.shape["space"], mesh.shape["vel"])
    return jax.shard_map(
        body, mesh=mesh, in_specs=placed, out_specs=P("space", None, None, "vel"), check_vma=False
    )
```

```python
import functools
import math

import jax
import jax.numpy as jnp
from jax import lax
from jax.experimental import pallas as pl
from jax.experimental.pallas import tpu as pltpu
from jax.sharding import PartitionSpec as P

VS = 16
LANE = 128
FEAT = 8
MOM = 16
MESH = pl.DeviceIdType.MESH

stream_x = 40.0
stream_y = 0.15
stream_z = 0.05
relaxation_multiplier = 0.05
shear_power_index = 0.81
diffusivity_ratio = 2.0 / 3.0

F32 = jnp.float32
BF16 = jnp.bfloat16


def rounded(x):
    return x.astype(BF16).astype(F32)


def velocity_rows(points):
    spacing = 8.0 / VS
    half = (VS - 1) / 2.0
    bits = VS.bit_length() - 1
    first = lax.shift_right_logical(points, 2 * bits).astype(F32)
    second = (lax.shift_right_logical(points, bits) & (VS - 1)).astype(F32)
    third = (points & (VS - 1)).astype(F32)
    return [(v - half) * spacing for v in (first, second, third)]


def stacked(rows, height):
    index = lax.broadcasted_iota(jnp.int32, (height, LANE), 0)
    out = jnp.zeros((height, LANE), F32)
    for k, row in enumerate(rows):
        out = jnp.where(index == k, row, out)
    return out


def kernel(
    dims,
    wall_mask,
    grid_ref,
    mirror_ref,
    f_hbm,
    out_ref,
    f_ref,
    wall_ref,
    wsplit_ref,
    pick_ref,
    cell_ref,
    eq_ref,
    mirrored_ref,
    fhi_ref,
    flo_ref,
    tmom_ref,
    gmat_ref,
    mom_ref,
    coef_ref,
    lhs_ref,
    rate_ref,
    prate_ref,
    rate_send,
    rate_recv,
    sa_ref,
    sb_ref,
    pb_ref,
    pair_a,
    pair_b,
    ed_ref,
    eu_ref,
    od_ref,
    ou_ref,
    enter_own,
    enter_send,
    enter_recv,
    f_sem,
    wall_ssem,
    wall_rsem,
    mom_ssem,
    mom_rsem,
    rate_sem,
    face_ssem,
    face_rsem,
    dn_ssem,
    dn_rsem,
    up_ssem,
    up_rsem,
    ret_ssem,
    ret_rsem,
):
    depth, rows, planes, blocks, nspace, nvel = dims
    stride = blocks * planes
    cells_x = planes * rows
    cells = depth * cells_x
    walls = depth * 2 * planes
    half_blocks = blocks // 2
    pairs = nspace // 2
    weight = (8.0 / VS) ** 3

    s = lax.axis_index("space")
    v = lax.axis_index("vel")
    q = lax.rem(s, 2)
    p = lax.div(s, 2)
    partner = s + 1 - 2 * q
    own0 = q * half_blocks
    far0 = (1 - q) * half_blocks

    def frow(x, y, j, z):
        return (x * rows + y) * stride + j * planes + z

    load = pltpu.make_async_copy(f_hbm, f_ref, f_sem)
    load.start()

    barrier = pltpu.get_barrier_semaphore()
    for d in range(1, nvel):
        pl.semaphore_signal(
            barrier, inc=1, device_id=(s, lax.rem(v + d, nvel)), device_id_type=MESH
        )
    pl.semaphore_signal(barrier, inc=1, device_id=(partner, v), device_id_type=MESH)

    @pl.when(p > 0)
    def _():
        pl.semaphore_signal(barrier, inc=1, device_id=(s - 2, v), device_id_type=MESH)

    @pl.when(p < pairs - 1)
    def _():
        pl.semaphore_signal(barrier, inc=1, device_id=(s + 2, v), device_id_type=MESH)

    tmom_ref[...] = jnp.zeros_like(tmom_ref)
    gmat_ref[...] = jnp.zeros_like(gmat_ref)
    coef_ref[...] = jnp.zeros_like(coef_ref)
    for j in range(blocks):
        x1, x2, x3 = velocity_rows(grid_ref[j : j + 1, :])
        one = jnp.ones_like(x1)
        square = x1 * x1 + x2 * x2 + x3 * x3
        cubic = [x * square for x in (x1, x2, x3)]
        cubic_hi = [rounded(x) for x in cubic]
        cubic_lo = [x - h for x, h in zip(cubic, cubic_hi)]
        table = [one, x1, x2, x3, x1 * x1, x2 * x2, x3 * x3, x1 * x2, x1 * x3, x2 * x3]
        tmom_ref[0:MOM, j * LANE : (j + 1) * LANE] = stacked(
            table + cubic_hi + cubic_lo, MOM
        ).astype(BF16)
        feat = stacked(table[:7], FEAT)
        zero = jnp.zeros_like(feat)
        for g in range(3):
            column = [zero] * 9
            for part in range(3):
                column[3 * part + g] = feat
            column = column + [zero]
            gmat_ref[j, 0 : 10 * FEAT, g * LANE : (g + 1) * LANE] = jnp.concatenate(
                column, axis=0
            ).astype(BF16)

        slot = mirror_ref[j : j + 1, :]
        index = lax.broadcasted_iota(jnp.int32, (2 * LANE, LANE), 0) & (LANE - 1)
        pick_ref[j] = jnp.where(index == (slot & (LANE - 1)), 1.0, 0.0).astype(BF16)

    load.wait()

    for x in range(depth):
        for w in range(2):
            for z in range(planes):
                r = (x * 2 + w) * planes + z
                y = (rows - 1) * w
                wall_ref[v, pl.ds(r, blocks, stride=walls), :] = f_ref[
                    pl.ds(frow(x, y, 0, z), blocks, stride=planes), :
                ]

    for x in range(depth):
        for z in range(planes):
            base = (x * planes + z) * rows
            for j in range(blocks):
                part = f_ref[pl.ds(frow(x, 0, j, z), rows, stride=stride), :]
                hi = part.astype(BF16)
                lo = (part - hi.astype(F32)).astype(BF16)
                cell_ref[j, x, z * rows : (z + 1) * rows, :] = part
                fhi_ref[base : base + rows, j * LANE : (j + 1) * LANE] = hi
                flo_ref[base : base + rows, j * LANE : (j + 1) * LANE] = lo

    greetings = nvel + (p > 0).astype(jnp.int32) + (p < pairs - 1).astype(jnp.int32)
    pl.semaphore_wait(barrier, greetings)

    sibling = v + 1 - 2 * lax.rem(v, 2)
    twins = nvel // 2

    def far(base, m):
        return lax.rem(base + 2 * m + nvel, nvel)

    def wall_copy(k, origin, target):
        return pltpu.make_async_remote_copy(
            src_ref=wall_ref.at[origin],
            dst_ref=wall_ref.at[origin],
            send_sem=wall_ssem.at[k],
            recv_sem=wall_rsem.at[k],
            device_id=(s, target),
            device_id_type=MESH,
        )

    def wall_far(m):
        return wall_copy(m, v, far(v, m))

    def wall_far_arrival(m):
        return wall_copy(m, far(v, -m), far(v, m))

    def wall_forward(m):
        return wall_copy(twins - 1 + m, far(v, -m), sibling)

    def wall_forward_arrival(m):
        return wall_copy(twins - 1 + m, far(sibling, -m), sibling)

    def mom_copy(k):
        target = far(v if k % 2 == 0 else sibling, k // 2)
        return pltpu.make_async_remote_copy(
            src_ref=mom_ref.at[0],
            dst_ref=mom_ref.at[k],
            send_sem=mom_ssem.at[k - 1],
            recv_sem=mom_rsem.at[k - 1],
            device_id=(s, target),
            device_id_type=MESH,
        )

    for m in range(1, twins):
        wall_far(m).start()
    wall_copy(0, v, sibling).start()

    contract = (((1,), (1,)), ((), ()))
    sums = lax.dot_general(
        fhi_ref[...], tmom_ref[...], contract, preferred_element_type=F32
    ) + lax.dot_general(flo_ref[...], tmom_ref[...], contract, preferred_element_type=F32)
    mom_ref[0] = sums.T[0:MOM, :]
    for d in range(nvel - 1, 0, -1):
        mom_copy(d).start()
    for m in range(1, twins):
        wall_far_arrival(m).wait_recv()
        wall_forward(m).start()
    row_index = lax.broadcasted_iota(jnp.int32, (rows, LANE), 0)

    def block_tables(j):
        return velocity_rows(grid_ref[pl.ds(j, 1), :])

    def flux_block(j, carry):
        _, x2, x3 = block_tables(j)
        pos2 = x2 > 0
        pos3 = x3 > 0
        coef_y = stream_y * jnp.abs(x2)
        coef_z = stream_z * jnp.abs(x3)
        coef_f = 1.0 - coef_y - coef_z
        for x in range(depth):
            values = [
                cell_ref[j, x, z * rows : (z + 1) * rows, :] for z in range(planes)
            ]
            for z in range(planes):
                below = jnp.where(row_index == 0, 0.0, pltpu.roll(values[z], 1, axis=0))
                above = jnp.where(
                    row_index == rows - 1, 0.0, pltpu.roll(values[z], rows - 1, axis=0)
                )
                side = jnp.where(pos2, below, above)
                before, after = values[(z - 1) % planes], values[(z + 1) % planes]
                if (z - 1) % planes == (z + 1) % planes:
                    plane = before
                else:
                    plane = jnp.where(pos3, before, after)
                sb_ref[j, x, z * rows : (z + 1) * rows, :] = (
                    coef_f * values[z] + coef_y * side + coef_z * plane
                )
        return carry

    lax.fori_loop(0, blocks, flux_block, 0)

    total = mom_ref[0]
    for d in range(1, nvel):
        mom_copy(d).wait_recv()
        total = total + mom_ref[d]
    total = total * weight

    raw = [total[k : k + 1, :] for k in range(MOM)]
    density = raw[0]
    momentum = raw[1:4]
    flow = [m / density for m in momentum]
    tensor = [[raw[4], raw[7], raw[8]], [raw[7], raw[5], raw[9]], [raw[8], raw[9], raw[6]]]
    third = [raw[10 + k] + raw[13 + k] for k in range(3)]
    trace = raw[4] + raw[5] + raw[6]
    flow_sq = flow[0] * flow[0] + flow[1] * flow[1] + flow[2] * flow[2]
    temperature = (trace - density * flow_sq) / (3.0 * density)
    flow_mom = flow[0] * momentum[0] + flow[1] * momentum[1] + flow[2] * momentum[2]
    heat = []
    for k in range(3):
        contracted = flow[0] * tensor[k][0] + flow[1] * tensor[k][1] + flow[2] * tensor[k][2]
        heat.append(
            0.5
            * (
                third[k]
                - 2.0 * contracted
                + flow_sq * momentum[k]
                - flow[k] * trace
                + 2.0 * flow[k] * flow_mom
                - flow[k] * flow_sq * density
            )
        )
    log_t = jnp.log(temperature)
    inverse_t = 1.0 / temperature
    rate = relaxation_multiplier * density * jnp.exp((1.0 - shear_power_index) * log_t)

    rate_send[...] = jnp.broadcast_to(rate, rate_send.shape)

    def rate_copy():
        return pltpu.make_async_remote_copy(
            src_ref=rate_send,
            dst_ref=rate_recv,
            send_sem=rate_sem.at[0],
            recv_sem=rate_sem.at[1],
            device_id=(partner, v),
            device_id_type=MESH,
        )

    rate_copy().start()
    scale = (1.0 - diffusivity_ratio) / 5.0 * inverse_t * inverse_t / density
    flow_heat = flow[0] * heat[0] + flow[1] * heat[1] + flow[2] * heat[2]
    exponent = [
        jnp.log(density) - 1.5 * (log_t + math.log(2.0 * math.pi)) - 0.5 * flow_sq * inverse_t
    ]
    exponent += [u * inverse_t for u in flow] + [-0.5 * inverse_t] * 3
    linear = [-scale * flow_heat] + [scale * h for h in heat]
    bracket = [flow_sq * inverse_t - 5.0]
    bracket += [-2.0 * u * inverse_t for u in flow] + [inverse_t] * 3
    for g, group in enumerate((exponent, linear, bracket)):
        for k, row in enumerate(group):
            coef_ref[g * FEAT + k : g * FEAT + k + 1, :] = row
    whole = coef_ref[0 : 3 * FEAT, :]
    hi = rounded(whole)
    mid = rounded(whole - hi)
    coef_ref[0 : 3 * FEAT, :] = hi
    coef_ref[3 * FEAT : 6 * FEAT, :] = mid
    coef_ref[6 * FEAT : 9 * FEAT, :] = whole - hi - mid
    lhs_ref[...] = coef_ref[...].T.astype(BF16)
    rate_ref[...] = jnp.broadcast_to(rate, (LANE, cells)).T

    for j in range(blocks):
        got = jnp.dot(lhs_ref[...], gmat_ref[j], preferred_element_type=F32)
        eq_ref[j] = jnp.exp(got[:, :LANE]) * (
            1.0 + got[:, LANE : 2 * LANE] * got[:, 2 * LANE :]
        )

    wall_copy(0, sibling, sibling).wait_recv()
    for m in range(1, twins):
        wall_forward_arrival(m).wait_recv()
    everywhere = wall_ref[...].reshape(nvel * blocks * walls, LANE)
    whi = everywhere.astype(BF16)
    wsplit_ref[:, :LANE] = whi
    wsplit_ref[:, LANE:] = (everywhere - whi.astype(F32)).astype(BF16)
    for j in range(blocks):
        high = lax.shift_right_logical(mirror_ref[j : j + 1, :], LANE.bit_length() - 1)
        found = jnp.dot(wsplit_ref[...], pick_ref[j], preferred_element_type=F32)
        acc = jnp.zeros((walls, LANE), F32)
        for h in range(nvel * blocks):
            acc = acc + jnp.where(high == h, found[h * walls : (h + 1) * walls], 0.0)
        mirrored_ref[j] = acc

    first_edge = jnp.where(s == 0, 1.0, 0.0).astype(F32)
    last_edge = jnp.where(s == nspace - 1, 1.0, 0.0).astype(F32)
    def local_block(j):
        x1, x2, _ = block_tables(j)
        pos1 = x1 > 0
        pos2 = x2 > 0
        coef_y = stream_y * jnp.abs(x2)
        coef_low = jnp.where(pos2, coef_y, 0.0)
        coef_high = jnp.where(pos2, 0.0, coef_y)
        sigma = stream_x * jnp.abs(x1)
        opening = 1.0 + sigma
        edge = jnp.where(pos1, first_edge, last_edge)
        mirrored = mirrored_ref[j]
        group_index = lax.broadcasted_iota(jnp.int32, (8, LANE), 0)
        a_list, b_list, eq_list = [], [], []
        for x in range(depth):
            base = x * cells_x
            equilibrium = eq_ref[j, base : base + cells_x, :]
            rates = rate_ref[base : base + cells_x, :]
            inverse = 1.0 / (opening + rates)
            parts = []
            for z in range(planes):
                low = (x * 2) * planes + z
                high = (x * 2 + 1) * planes + z
                mask_low = jnp.full((1, LANE), wall_mask[0, z, x])
                mask_high = jnp.full((1, LANE), wall_mask[1, z, x])
                eq_z = equilibrium[z * rows : (z + 1) * rows]
                ghost_low = jnp.where(mask_low == 1, mirrored[low : low + 1], eq_z[0:1])
                ghost_high = jnp.where(
                    mask_high == 1, mirrored[high : high + 1], eq_z[rows - 1 : rows]
                )
                flux = sb_ref[j, x, z * rows : (z + 1) * rows, :]
                parts += [
                    flux[:8] + jnp.where(group_index == 0, coef_low * ghost_low, 0.0),
                    flux[8 : rows - 8],
                    flux[rows - 8 :] + jnp.where(group_index == 7, coef_high * ghost_high, 0.0),
                ]
            b_list.append((jnp.concatenate(parts, axis=0) + rates * equilibrium) * inverse)
            a_list.append(sigma * inverse)
            if x in (0, depth - 1):
                eq_list.append(equilibrium)
        a_run = b_run = None
        for k in range(depth):
            a_k = jnp.where(pos1, a_list[k], a_list[depth - 1 - k])
            b_k = jnp.where(pos1, b_list[k], b_list[depth - 1 - k])
            if k == 0:
                target = jnp.where(pos1, eq_list[0], eq_list[-1])
                b_run = b_k + a_k * (edge * target)
                a_run = a_k * (1.0 - edge)
            else:
                b_run = a_k * b_run + b_k
                a_run = a_k * a_run
            sa_ref[j, k] = a_run
            sb_ref[j, k] = b_run

    def band(z):
        return pl.ds(z * rows, rows)

    def face_copy(c, z):
        return pltpu.make_async_remote_copy(
            src_ref=sb_ref.at[far0 + c, depth - 1, band(z)],
            dst_ref=pb_ref.at[c, band(z)],
            send_sem=face_ssem.at[c, z],
            recv_sem=face_rsem.at[c, z],
            device_id=(partner, v),
            device_id_type=MESH,
        )

    def far_block(c, carry):
        local_block(far0 + c)
        for z in range(planes):
            face_copy(c, z).start()

        @pl.when(c > 0)
        def _():
            local_block(own0 + c - 1)

        return carry

    lax.fori_loop(0, half_blocks, far_block, 0)
    local_block(own0 + half_blocks - 1)

    rate_copy().wait()
    prate_ref[...] = jnp.broadcast_to(rate_recv[0:1, :], (LANE, cells)).T


    def first_weight(x1):
        sign = jnp.where(x1 > 0, 1.0, -1.0)
        return sign * jnp.where(q == 0, 1.0, -1.0) > 0

    def pair_block(c):
        j = own0 + c
        x1, _, _ = block_tables(j)
        sigma = stream_x * jnp.abs(x1)
        opening = 1.0 + sigma
        other = None
        for x in range(depth):
            a = sigma / (opening + prate_ref[x * cells_x : (x + 1) * cells_x, :])
            other = a if other is None else other * a
        for z in range(planes):
            face_copy(c, z).wait_recv()
        a_own = sa_ref[j, depth - 1]
        b_own = sb_ref[j, depth - 1]
        b_other = pb_ref[c]
        first = first_weight(x1)
        pair_a[c, 0] = other
        pair_a[c, 1] = a_own * other
        pair_b[c] = jnp.where(first, other * b_own + b_other, a_own * b_other + b_own)

    def down_copy(c, z):
        return pltpu.make_async_remote_copy(
            src_ref=od_ref.at[c, band(z)],
            dst_ref=ed_ref.at[c, band(z)],
            send_sem=dn_ssem.at[c, z],
            recv_sem=dn_rsem.at[c, z],
            device_id=(s + 2, v),
            device_id_type=MESH,
        )

    def up_copy(c, z):
        return pltpu.make_async_remote_copy(
            src_ref=ou_ref.at[c, band(z)],
            dst_ref=eu_ref.at[c, band(z)],
            send_sem=up_ssem.at[c, z],
            recv_sem=up_rsem.at[c, z],
            device_id=(s - 2, v),
            device_id_type=MESH,
        )

    def return_copy(c, z):
        return pltpu.make_async_remote_copy(
            src_ref=enter_send.at[c, band(z)],
            dst_ref=enter_recv.at[c, band(z)],
            send_sem=ret_ssem.at[c, z],
            recv_sem=ret_rsem.at[c, z],
            device_id=(partner, v),
            device_id_type=MESH,
        )

    @pl.when(p == 0)
    def _():
        ed_ref[...] = jnp.zeros_like(ed_ref)

    @pl.when(p == pairs - 1)
    def _():
        eu_ref[...] = jnp.zeros_like(eu_ref)

    back = pairs - 1 - p
    latest = jnp.maximum(p, back)

    def chain_step(t, carry):
        c_dn = t - p
        c_up = t - back
        c_end = t - latest

        @pl.when(t < half_blocks)
        def _():
            pair_block(t)

        @pl.when((c_dn >= 0) & (c_dn < half_blocks))
        def _():
            for z in range(planes):
                at = (c_dn, band(z))

                @pl.when(p > 0)
                def _():
                    down_copy(c_dn, z).wait_recv()

                @pl.when(p < pairs - 1)
                def _():
                    od_ref[at] = pair_a[c_dn, 1, band(z)] * ed_ref[at] + pair_b[at]
                    down_copy(c_dn, z).start()

        @pl.when((c_up >= 0) & (c_up < half_blocks))
        def _():
            for z in range(planes):
                at = (c_up, band(z))

                @pl.when(p < pairs - 1)
                def _():
                    up_copy(c_up, z).wait_recv()

                @pl.when(p > 0)
                def _():
                    ou_ref[at] = pair_a[c_up, 1, band(z)] * eu_ref[at] + pair_b[at]
                    up_copy(c_up, z).start()

        @pl.when((c_end >= 0) & (c_end < half_blocks))
        def _():
            j = own0 + c_end
            x1, _, _ = block_tables(j)
            first = first_weight(x1)
            for z in range(planes):
                at = (c_end, band(z))
                enter = jnp.where(x1 > 0, ed_ref[at], eu_ref[at])
                last = (j, depth - 1, band(z))
                after_own = sa_ref[last] * enter + sb_ref[last]
                after_other = pair_a[c_end, 0, band(z)] * enter + pb_ref[at]
                enter_send[at] = jnp.where(first, after_own, enter)
                return_copy(c_end, z).start()
                enter_own[at] = jnp.where(first, enter, after_other)

        return carry

    lax.fori_loop(0, half_blocks + pairs - 1, chain_step, 0)

    def finish(j, enter):
        x1, _, _ = block_tables(j)
        pos1 = x1 > 0
        done = [sa_ref[j, k] * enter + sb_ref[j, k] for k in range(depth)]
        for x in range(depth):
            value = jnp.where(pos1, done[x], done[depth - 1 - x])
            for z in range(planes):
                out_ref[pl.ds(frow(x, 0, j, z), rows, stride=stride), :] = value[
                    z * rows : (z + 1) * rows
                ]

    def finish_own(c, carry):
        finish(own0 + c, enter_own[c])
        return carry

    def finish_far(c, carry):
        for z in range(planes):
            return_copy(c, z).wait_recv()
        finish(far0 + c, enter_recv[c])
        return carry

    lax.fori_loop(0, half_blocks, finish_own, 0)
    lax.fori_loop(0, half_blocks, finish_far, 0)

    wall_copy(0, v, sibling).wait_send()
    for m in range(1, twins):
        wall_far(m).wait_send()
        wall_forward(m).wait_send()
    for d in range(1, nvel):
        mom_copy(d).wait_send()

    def drain(c, carry):
        for z in range(planes):
            face_copy(c, z).wait_send()
            return_copy(c, z).wait_send()

            @pl.when(p < pairs - 1)
            def _():
                down_copy(c, z).wait_send()

            @pl.when(p > 0)
            def _():
                up_copy(c, z).wait_send()

        return carry

    lax.fori_loop(0, half_blocks, drain, 0)


def shards(nspace, nvel, distribution, wall_mask, grid_point, mirror_slot):
    depth, rows, planes, width = distribution.shape
    blocks = width // LANE
    half = blocks // 2
    dims = (depth, rows, planes, blocks, nspace, nvel)
    count = depth * rows * planes * blocks
    stride = blocks * planes
    side = planes * rows
    cells = depth * side
    walls = depth * 2 * planes
    flat = (
        distribution.reshape(depth, rows, planes, blocks, LANE)
        .transpose(0, 1, 3, 2, 4)
        .reshape(count, LANE)
    )
    vmem = pl.BlockSpec(memory_space=pltpu.VMEM)
    face = (half, side, LANE)
    out = pl.pallas_call(
        functools.partial(kernel, dims),
        out_shape=jax.ShapeDtypeStruct((count, LANE), F32),
        in_specs=[
            pl.BlockSpec(memory_space=pltpu.SMEM),
            vmem,
            vmem,
            pl.BlockSpec(memory_space=pl.ANY),
        ],
        out_specs=vmem,
        scratch_shapes=[
            pltpu.VMEM((count, LANE), F32),
            pltpu.VMEM((nvel, blocks * walls, LANE), F32),
            pltpu.VMEM((nvel * blocks * walls, 2 * LANE), BF16),
            pltpu.VMEM((blocks, 2 * LANE, LANE), BF16),
            pltpu.VMEM((blocks, depth, side, LANE), F32),
            pltpu.VMEM((blocks, cells, LANE), F32),
            pltpu.VMEM((blocks, walls, LANE), F32),
            pltpu.VMEM((cells, width), BF16),
            pltpu.VMEM((cells, width), BF16),
            pltpu.VMEM((LANE, width), BF16),
            pltpu.VMEM((blocks, LANE, 3 * LANE), BF16),
            pltpu.VMEM((nvel, MOM, cells), F32),
            pltpu.VMEM((LANE, cells), F32),
            pltpu.VMEM((cells, LANE), BF16),
            pltpu.VMEM((cells, LANE), F32),
            pltpu.VMEM((cells, LANE), F32),
            pltpu.VMEM((8, cells), F32),
            pltpu.VMEM((8, cells), F32),
            pltpu.VMEM((blocks, depth, side, LANE), F32),
            pltpu.VMEM((blocks, depth, side, LANE), F32),
            pltpu.VMEM(face, F32),
            pltpu.VMEM((half, 2, side, LANE), F32),
            pltpu.VMEM(face, F32),
            pltpu.VMEM(face, F32),
            pltpu.VMEM(face, F32),
            pltpu.VMEM(face, F32),
            pltpu.VMEM(face, F32),
            pltpu.VMEM(face, F32),
            pltpu.VMEM(face, F32),
            pltpu.VMEM(face, F32),
            pltpu.SemaphoreType.DMA,
            pltpu.SemaphoreType.DMA((nvel - 1,)),
            pltpu.SemaphoreType.DMA((nvel - 1,)),
            pltpu.SemaphoreType.DMA((nvel - 1,)),
            pltpu.SemaphoreType.DMA((nvel - 1,)),
            pltpu.SemaphoreType.DMA((2,)),
        ]
        + [pltpu.SemaphoreType.DMA((half, planes))] * 8,
        compiler_params=pltpu.CompilerParams(
            collective_id=0, has_side_effects=True, vmem_limit_bytes=62 * 1024 * 1024
        ),
    )(wall_mask.transpose(1, 2, 0), grid_point.reshape(blocks, LANE), mirror_slot.reshape(blocks, LANE), flat)
    return (
        out.reshape(depth, rows, blocks, planes, LANE)
        .transpose(0, 1, 3, 2, 4)
        .reshape(depth, rows, planes, width)
    )


def solution(mesh):
    placed = (P("space", None, None, "vel"), P("space", None, None), P("vel"), P("vel"))
    body = functools.partial(shards, mesh.shape["space"], mesh.shape["vel"])
    return jax.shard_map(
        body, mesh=mesh, in_specs=placed, out_specs=P("space", None, None, "vel"), check_vma=False
    )
```

```python
import functools
import math

import jax
import jax.numpy as jnp
from jax import lax
from jax.experimental import pallas as pl
from jax.experimental.pallas import tpu as pltpu
from jax.sharding import PartitionSpec as P

VS = 16
LANE = 128
FEAT = 8
MOM = 16
MESH = pl.DeviceIdType.MESH

stream_x = 40.0
stream_y = 0.15
stream_z = 0.05
relaxation_multiplier = 0.05
shear_power_index = 0.81
diffusivity_ratio = 2.0 / 3.0

F32 = jnp.float32
BF16 = jnp.bfloat16


def rounded(x):
    return x.astype(BF16).astype(F32)


def velocity_rows(points):
    spacing = 8.0 / VS
    half = (VS - 1) / 2.0
    bits = VS.bit_length() - 1
    first = lax.shift_right_logical(points, 2 * bits).astype(F32)
    second = (lax.shift_right_logical(points, bits) & (VS - 1)).astype(F32)
    third = (points & (VS - 1)).astype(F32)
    return [(v - half) * spacing for v in (first, second, third)]


def stacked(rows, height):
    index = lax.broadcasted_iota(jnp.int32, (height, LANE), 0)
    out = jnp.zeros((height, LANE), F32)
    for k, row in enumerate(rows):
        out = jnp.where(index == k, row, out)
    return out


def kernel(
    dims,
    wall_mask,
    grid_ref,
    mirror_ref,
    f_hbm,
    out_ref,
    f_ref,
    wall_ref,
    wsplit_ref,
    pick_ref,
    cell_ref,
    eq_ref,
    mirrored_ref,
    fhi_ref,
    flo_ref,
    tmom_ref,
    gmat_ref,
    mom_ref,
    coef_ref,
    lhs_ref,
    rate_ref,
    prate_ref,
    rate_send,
    rate_recv,
    sa_ref,
    sb_ref,
    pb_ref,
    pair_a,
    pair_b,
    ed_ref,
    eu_ref,
    od_ref,
    ou_ref,
    enter_own,
    enter_send,
    enter_recv,
    f_sem,
    wall_ssem,
    wall_rsem,
    mom_ssem,
    mom_rsem,
    rate_sem,
    face_ssem,
    face_rsem,
    dn_ssem,
    dn_rsem,
    up_ssem,
    up_rsem,
    ret_ssem,
    ret_rsem,
):
    depth, rows, planes, blocks, nspace, nvel = dims
    stride = blocks * planes
    cells_x = planes * rows
    cells = depth * cells_x
    walls = depth * 2 * planes
    half_blocks = blocks // 2
    pairs = nspace // 2
    weight = (8.0 / VS) ** 3

    s = lax.axis_index("space")
    v = lax.axis_index("vel")
    q = lax.rem(s, 2)
    p = lax.div(s, 2)
    partner = s + 1 - 2 * q
    own0 = q * half_blocks
    far0 = (1 - q) * half_blocks

    def frow(x, y, j, z):
        return (x * rows + y) * stride + j * planes + z

    load = pltpu.make_async_copy(f_hbm, f_ref, f_sem)
    load.start()

    barrier = pltpu.get_barrier_semaphore()
    for d in range(1, nvel):
        pl.semaphore_signal(
            barrier, inc=1, device_id=(s, lax.rem(v + d, nvel)), device_id_type=MESH
        )
    pl.semaphore_signal(barrier, inc=1, device_id=(partner, v), device_id_type=MESH)

    @pl.when(p > 0)
    def _():
        pl.semaphore_signal(barrier, inc=1, device_id=(s - 2, v), device_id_type=MESH)

    @pl.when(p < pairs - 1)
    def _():
        pl.semaphore_signal(barrier, inc=1, device_id=(s + 2, v), device_id_type=MESH)

    tmom_ref[...] = jnp.zeros_like(tmom_ref)
    gmat_ref[...] = jnp.zeros_like(gmat_ref)
    coef_ref[...] = jnp.zeros_like(coef_ref)
    for j in range(blocks):
        x1, x2, x3 = velocity_rows(grid_ref[j : j + 1, :])
        one = jnp.ones_like(x1)
        square = x1 * x1 + x2 * x2 + x3 * x3
        cubic = [x * square for x in (x1, x2, x3)]
        cubic_hi = [rounded(x) for x in cubic]
        cubic_lo = [x - h for x, h in zip(cubic, cubic_hi)]
        table = [one, x1, x2, x3, x1 * x1, x2 * x2, x3 * x3, x1 * x2, x1 * x3, x2 * x3]
        tmom_ref[0:MOM, j * LANE : (j + 1) * LANE] = stacked(
            table + cubic_hi + cubic_lo, MOM
        ).astype(BF16)
        feat = stacked(table[:7], FEAT)
        zero = jnp.zeros_like(feat)
        for g in range(3):
            column = [zero] * 9
            for part in range(3):
                column[3 * part + g] = feat
            column = column + [zero]
            gmat_ref[j, 0 : 10 * FEAT, g * LANE : (g + 1) * LANE] = jnp.concatenate(
                column, axis=0
            ).astype(BF16)

        slot = mirror_ref[j : j + 1, :]
        index = lax.broadcasted_iota(jnp.int32, (2 * LANE, LANE), 0) & (LANE - 1)
        pick_ref[j] = jnp.where(index == (slot & (LANE - 1)), 1.0, 0.0).astype(BF16)

    load.wait()

    for x in range(depth):
        for w in range(2):
            for z in range(planes):
                r = (x * 2 + w) * planes + z
                y = (rows - 1) * w
                wall_ref[v, pl.ds(r, blocks, stride=walls), :] = f_ref[
                    pl.ds(frow(x, y, 0, z), blocks, stride=planes), :
                ]

    for x in range(depth):
        for z in range(planes):
            base = (x * planes + z) * rows
            for j in range(blocks):
                part = f_ref[pl.ds(frow(x, 0, j, z), rows, stride=stride), :]
                hi = part.astype(BF16)
                lo = (part - hi.astype(F32)).astype(BF16)
                cell_ref[j, x, z * rows : (z + 1) * rows, :] = part
                fhi_ref[base : base + rows, j * LANE : (j + 1) * LANE] = hi
                flo_ref[base : base + rows, j * LANE : (j + 1) * LANE] = lo

    greetings = nvel + (p > 0).astype(jnp.int32) + (p < pairs - 1).astype(jnp.int32)
    pl.semaphore_wait(barrier, greetings)

    sibling = v + 1 - 2 * lax.rem(v, 2)
    twins = nvel // 2

    def far(base, m):
        return lax.rem(base + 2 * m + nvel, nvel)

    def wall_copy(k, origin, target):
        return pltpu.make_async_remote_copy(
            src_ref=wall_ref.at[origin],
            dst_ref=wall_ref.at[origin],
            send_sem=wall_ssem.at[k],
            recv_sem=wall_rsem.at[k],
            device_id=(s, target),
            device_id_type=MESH,
        )

    def wall_far(m):
        return wall_copy(m, v, far(v, m))

    def wall_far_arrival(m):
        return wall_copy(m, far(v, -m), far(v, m))

    def wall_forward(m):
        return wall_copy(twins - 1 + m, far(v, -m), sibling)

    def wall_forward_arrival(m):
        return wall_copy(twins - 1 + m, far(sibling, -m), sibling)

    def mom_copy(k):
        target = far(v if k % 2 == 0 else sibling, k // 2)
        return pltpu.make_async_remote_copy(
            src_ref=mom_ref.at[0],
            dst_ref=mom_ref.at[k],
            send_sem=mom_ssem.at[k - 1],
            recv_sem=mom_rsem.at[k - 1],
            device_id=(s, target),
            device_id_type=MESH,
        )

    for m in range(1, twins):
        wall_far(m).start()
    wall_copy(0, v, sibling).start()

    contract = (((1,), (1,)), ((), ()))
    sums = lax.dot_general(
        fhi_ref[...], tmom_ref[...], contract, preferred_element_type=F32
    ) + lax.dot_general(flo_ref[...], tmom_ref[...], contract, preferred_element_type=F32)
    mom_ref[0] = sums.T[0:MOM, :]
    for d in range(nvel - 1, 0, -1):
        mom_copy(d).start()
    for m in range(1, twins):
        wall_far_arrival(m).wait_recv()
        wall_forward(m).start()
    row_index = lax.broadcasted_iota(jnp.int32, (rows, LANE), 0)

    def block_tables(j):
        return velocity_rows(grid_ref[pl.ds(j, 1), :])

    def flux_block(j, carry):
        _, x2, x3 = block_tables(j)
        pos2 = x2 > 0
        pos3 = x3 > 0
        coef_y = stream_y * jnp.abs(x2)
        coef_z = stream_z * jnp.abs(x3)
        coef_f = 1.0 - coef_y - coef_z
        for x in range(depth):
            values = [
                cell_ref[j, x, z * rows : (z + 1) * rows, :] for z in range(planes)
            ]
            for z in range(planes):
                below = jnp.where(row_index == 0, 0.0, pltpu.roll(values[z], 1, axis=0))
                above = jnp.where(
                    row_index == rows - 1, 0.0, pltpu.roll(values[z], rows - 1, axis=0)
                )
                side = jnp.where(pos2, below, above)
                before, after = values[(z - 1) % planes], values[(z + 1) % planes]
                if (z - 1) % planes == (z + 1) % planes:
                    plane = before
                else:
                    plane = jnp.where(pos3, before, after)
                sb_ref[j, x, z * rows : (z + 1) * rows, :] = (
                    coef_f * values[z] + coef_y * side + coef_z * plane
                )
        return carry

    lax.fori_loop(0, blocks, flux_block, 0)

    total = mom_ref[0]
    for d in range(1, nvel):
        mom_copy(d).wait_recv()
        total = total + mom_ref[d]
    total = total * weight

    raw = [total[k : k + 1, :] for k in range(MOM)]
    density = raw[0]
    momentum = raw[1:4]
    flow = [m / density for m in momentum]
    tensor = [[raw[4], raw[7], raw[8]], [raw[7], raw[5], raw[9]], [raw[8], raw[9], raw[6]]]
    third = [raw[10 + k] + raw[13 + k] for k in range(3)]
    trace = raw[4] + raw[5] + raw[6]
    flow_sq = flow[0] * flow[0] + flow[1] * flow[1] + flow[2] * flow[2]
    temperature = (trace - density * flow_sq) / (3.0 * density)
    flow_mom = flow[0] * momentum[0] + flow[1] * momentum[1] + flow[2] * momentum[2]
    heat = []
    for k in range(3):
        contracted = flow[0] * tensor[k][0] + flow[1] * tensor[k][1] + flow[2] * tensor[k][2]
        heat.append(
            0.5
            * (
                third[k]
                - 2.0 * contracted
                + flow_sq * momentum[k]
                - flow[k] * trace
                + 2.0 * flow[k] * flow_mom
                - flow[k] * flow_sq * density
            )
        )
    log_t = jnp.log(temperature)
    inverse_t = 1.0 / temperature
    rate = relaxation_multiplier * density * jnp.exp((1.0 - shear_power_index) * log_t)

    rate_send[...] = jnp.broadcast_to(rate, rate_send.shape)

    def rate_copy():
        return pltpu.make_async_remote_copy(
            src_ref=rate_send,
            dst_ref=rate_recv,
            send_sem=rate_sem.at[0],
            recv_sem=rate_sem.at[1],
            device_id=(partner, v),
            device_id_type=MESH,
        )

    rate_copy().start()
    scale = (1.0 - diffusivity_ratio) / 5.0 * inverse_t * inverse_t / density
    flow_heat = flow[0] * heat[0] + flow[1] * heat[1] + flow[2] * heat[2]
    exponent = [
        jnp.log(density) - 1.5 * (log_t + math.log(2.0 * math.pi)) - 0.5 * flow_sq * inverse_t
    ]
    exponent += [u * inverse_t for u in flow] + [-0.5 * inverse_t] * 3
    linear = [-scale * flow_heat] + [scale * h for h in heat]
    bracket = [flow_sq * inverse_t - 5.0]
    bracket += [-2.0 * u * inverse_t for u in flow] + [inverse_t] * 3
    for g, group in enumerate((exponent, linear, bracket)):
        for k, row in enumerate(group):
            coef_ref[g * FEAT + k : g * FEAT + k + 1, :] = row
    whole = coef_ref[0 : 3 * FEAT, :]
    hi = rounded(whole)
    mid = rounded(whole - hi)
    coef_ref[0 : 3 * FEAT, :] = hi
    coef_ref[3 * FEAT : 6 * FEAT, :] = mid
    coef_ref[6 * FEAT : 9 * FEAT, :] = whole - hi - mid
    lhs_ref[...] = coef_ref[...].T.astype(BF16)
    rate_ref[...] = jnp.broadcast_to(rate, (LANE, cells)).T

    for j in range(blocks):
        got = jnp.dot(lhs_ref[...], gmat_ref[j], preferred_element_type=F32)
        eq_ref[j] = jnp.exp(got[:, :LANE]) * (
            1.0 + got[:, LANE : 2 * LANE] * got[:, 2 * LANE :]
        )

    wall_copy(0, sibling, sibling).wait_recv()
    for m in range(1, twins):
        wall_forward_arrival(m).wait_recv()
    everywhere = wall_ref[...].reshape(nvel * blocks * walls, LANE)
    whi = everywhere.astype(BF16)
    wsplit_ref[:, :LANE] = whi
    wsplit_ref[:, LANE:] = (everywhere - whi.astype(F32)).astype(BF16)
    for j in range(blocks):
        high = lax.shift_right_logical(mirror_ref[j : j + 1, :], LANE.bit_length() - 1)
        found = jnp.dot(wsplit_ref[...], pick_ref[j], preferred_element_type=F32)
        acc = jnp.zeros((walls, LANE), F32)
        for h in range(nvel * blocks):
            acc = acc + jnp.where(high == h, found[h * walls : (h + 1) * walls], 0.0)
        mirrored_ref[j] = acc

    first_edge = jnp.where(s == 0, 1.0, 0.0).astype(F32)
    last_edge = jnp.where(s == nspace - 1, 1.0, 0.0).astype(F32)
    def local_block(j):
        x1, x2, _ = block_tables(j)
        pos1 = x1 > 0
        pos2 = x2 > 0
        coef_y = stream_y * jnp.abs(x2)
        coef_low = jnp.where(pos2, coef_y, 0.0)
        coef_high = jnp.where(pos2, 0.0, coef_y)
        sigma = stream_x * jnp.abs(x1)
        opening = 1.0 + sigma
        edge = jnp.where(pos1, first_edge, last_edge)
        mirrored = mirrored_ref[j]
        group_index = lax.broadcasted_iota(jnp.int32, (8, LANE), 0)
        a_list, b_list, eq_list = [], [], []
        for x in range(depth):
            base = x * cells_x
            equilibrium = eq_ref[j, base : base + cells_x, :]
            rates = rate_ref[base : base + cells_x, :]
            inverse = 1.0 / (opening + rates)
            parts = []
            for z in range(planes):
                low = (x * 2) * planes + z
                high = (x * 2 + 1) * planes + z
                mask_low = jnp.full((1, LANE), wall_mask[0, z, x])
                mask_high = jnp.full((1, LANE), wall_mask[1, z, x])
                eq_z = equilibrium[z * rows : (z + 1) * rows]
                ghost_low = jnp.where(mask_low == 1, mirrored[low : low + 1], eq_z[0:1])
                ghost_high = jnp.where(
                    mask_high == 1, mirrored[high : high + 1], eq_z[rows - 1 : rows]
                )
                flux = sb_ref[j, x, z * rows : (z + 1) * rows, :]
                parts += [
                    flux[:8] + jnp.where(group_index == 0, coef_low * ghost_low, 0.0),
                    flux[8 : rows - 8],
                    flux[rows - 8 :] + jnp.where(group_index == 7, coef_high * ghost_high, 0.0),
                ]
            b_list.append((jnp.concatenate(parts, axis=0) + rates * equilibrium) * inverse)
            a_list.append(sigma * inverse)
            if x in (0, depth - 1):
                eq_list.append(equilibrium)
        a_run = b_run = None
        for k in range(depth):
            a_k = jnp.where(pos1, a_list[k], a_list[depth - 1 - k])
            b_k = jnp.where(pos1, b_list[k], b_list[depth - 1 - k])
            if k == 0:
                target = jnp.where(pos1, eq_list[0], eq_list[-1])
                b_run = b_k + a_k * (edge * target)
                a_run = a_k * (1.0 - edge)
            else:
                b_run = a_k * b_run + b_k
                a_run = a_k * a_run
            sa_ref[j, k] = a_run
            sb_ref[j, k] = b_run

    def band(z):
        return pl.ds(z * rows, rows)

    def face_copy(c, z):
        return pltpu.make_async_remote_copy(
            src_ref=sb_ref.at[far0 + c, depth - 1, band(z)],
            dst_ref=pb_ref.at[c, band(z)],
            send_sem=face_ssem.at[c, z],
            recv_sem=face_rsem.at[c, z],
            device_id=(partner, v),
            device_id_type=MESH,
        )

    def far_block(c, carry):
        local_block(far0 + c)
        for z in range(planes):
            face_copy(c, z).start()

        @pl.when(c > 0)
        def _():
            local_block(own0 + c - 1)

        return carry

    lax.fori_loop(0, half_blocks, far_block, 0)
    local_block(own0 + half_blocks - 1)

    rate_copy().wait()
    prate_ref[...] = jnp.broadcast_to(rate_recv[0:1, :], (LANE, cells)).T


    def first_weight(x1):
        sign = jnp.where(x1 > 0, 1.0, -1.0)
        return sign * jnp.where(q == 0, 1.0, -1.0) > 0

    def pair_block(c):
        j = own0 + c
        x1, _, _ = block_tables(j)
        sigma = stream_x * jnp.abs(x1)
        opening = 1.0 + sigma
        other = None
        for x in range(depth):
            a = sigma / (opening + prate_ref[x * cells_x : (x + 1) * cells_x, :])
            other = a if other is None else other * a
        for z in range(planes):
            face_copy(c, z).wait_recv()
        a_own = sa_ref[j, depth - 1]
        b_own = sb_ref[j, depth - 1]
        b_other = pb_ref[c]
        first = first_weight(x1)
        pair_a[c, 0] = other
        pair_a[c, 1] = a_own * other
        pair_b[c] = jnp.where(first, other * b_own + b_other, a_own * b_other + b_own)

    def down_copy(c, z):
        return pltpu.make_async_remote_copy(
            src_ref=od_ref.at[c, band(z)],
            dst_ref=ed_ref.at[c, band(z)],
            send_sem=dn_ssem.at[c, z],
            recv_sem=dn_rsem.at[c, z],
            device_id=(s + 2, v),
            device_id_type=MESH,
        )

    def up_copy(c, z):
        return pltpu.make_async_remote_copy(
            src_ref=ou_ref.at[c, band(z)],
            dst_ref=eu_ref.at[c, band(z)],
            send_sem=up_ssem.at[c, z],
            recv_sem=up_rsem.at[c, z],
            device_id=(s - 2, v),
            device_id_type=MESH,
        )

    def return_copy(c, z):
        return pltpu.make_async_remote_copy(
            src_ref=enter_send.at[c, band(z)],
            dst_ref=enter_recv.at[c, band(z)],
            send_sem=ret_ssem.at[c, z],
            recv_sem=ret_rsem.at[c, z],
            device_id=(partner, v),
            device_id_type=MESH,
        )

    @pl.when(p == 0)
    def _():
        ed_ref[...] = jnp.zeros_like(ed_ref)

    @pl.when(p == pairs - 1)
    def _():
        eu_ref[...] = jnp.zeros_like(eu_ref)

    def finish(j, enter):
        x1, _, _ = block_tables(j)
        pos1 = x1 > 0
        done = [sa_ref[j, k] * enter + sb_ref[j, k] for k in range(depth)]
        for x in range(depth):
            value = jnp.where(pos1, done[x], done[depth - 1 - x])
            for z in range(planes):
                out_ref[pl.ds(frow(x, 0, j, z), rows, stride=stride), :] = value[
                    z * rows : (z + 1) * rows
                ]

    back = pairs - 1 - p
    latest = jnp.maximum(p, back)

    def chain_step(t, carry):
        c_dn = t - p
        c_up = t - back
        c_end = t - latest

        @pl.when(t < half_blocks)
        def _():
            pair_block(t)

        @pl.when((c_dn >= 0) & (c_dn < half_blocks))
        def _():
            for z in range(planes):
                at = (c_dn, band(z))

                @pl.when(p > 0)
                def _():
                    down_copy(c_dn, z).wait_recv()

                @pl.when(p < pairs - 1)
                def _():
                    od_ref[at] = pair_a[c_dn, 1, band(z)] * ed_ref[at] + pair_b[at]
                    down_copy(c_dn, z).start()

        @pl.when((c_up >= 0) & (c_up < half_blocks))
        def _():
            for z in range(planes):
                at = (c_up, band(z))

                @pl.when(p < pairs - 1)
                def _():
                    up_copy(c_up, z).wait_recv()

                @pl.when(p > 0)
                def _():
                    ou_ref[at] = pair_a[c_up, 1, band(z)] * eu_ref[at] + pair_b[at]
                    up_copy(c_up, z).start()

        @pl.when((c_end >= 0) & (c_end < half_blocks))
        def _():
            j = own0 + c_end
            x1, _, _ = block_tables(j)
            first = first_weight(x1)
            for z in range(planes):
                at = (c_end, band(z))
                enter = jnp.where(x1 > 0, ed_ref[at], eu_ref[at])
                last = (j, depth - 1, band(z))
                after_own = sa_ref[last] * enter + sb_ref[last]
                after_other = pair_a[c_end, 0, band(z)] * enter + pb_ref[at]
                enter_send[at] = jnp.where(first, after_own, enter)
                return_copy(c_end, z).start()
                enter_own[at] = jnp.where(first, enter, after_other)
            finish(j, enter_own[c_end])

        return carry

    lax.fori_loop(0, half_blocks + pairs - 1, chain_step, 0)

    def finish_far(c, carry):
        for z in range(planes):
            return_copy(c, z).wait_recv()
        finish(far0 + c, enter_recv[c])
        return carry

    lax.fori_loop(0, half_blocks, finish_far, 0)

    wall_copy(0, v, sibling).wait_send()
    for m in range(1, twins):
        wall_far(m).wait_send()
        wall_forward(m).wait_send()
    for d in range(1, nvel):
        mom_copy(d).wait_send()

    def drain(c, carry):
        for z in range(planes):
            face_copy(c, z).wait_send()
            return_copy(c, z).wait_send()

            @pl.when(p < pairs - 1)
            def _():
                down_copy(c, z).wait_send()

            @pl.when(p > 0)
            def _():
                up_copy(c, z).wait_send()

        return carry

    lax.fori_loop(0, half_blocks, drain, 0)


def shards(nspace, nvel, distribution, wall_mask, grid_point, mirror_slot):
    depth, rows, planes, width = distribution.shape
    blocks = width // LANE
    half = blocks // 2
    dims = (depth, rows, planes, blocks, nspace, nvel)
    count = depth * rows * planes * blocks
    stride = blocks * planes
    side = planes * rows
    cells = depth * side
    walls = depth * 2 * planes
    flat = (
        distribution.reshape(depth, rows, planes, blocks, LANE)
        .transpose(0, 1, 3, 2, 4)
        .reshape(count, LANE)
    )
    vmem = pl.BlockSpec(memory_space=pltpu.VMEM)
    face = (half, side, LANE)
    out = pl.pallas_call(
        functools.partial(kernel, dims),
        out_shape=jax.ShapeDtypeStruct((count, LANE), F32),
        in_specs=[
            pl.BlockSpec(memory_space=pltpu.SMEM),
            vmem,
            vmem,
            pl.BlockSpec(memory_space=pl.ANY),
        ],
        out_specs=vmem,
        scratch_shapes=[
            pltpu.VMEM((count, LANE), F32),
            pltpu.VMEM((nvel, blocks * walls, LANE), F32),
            pltpu.VMEM((nvel * blocks * walls, 2 * LANE), BF16),
            pltpu.VMEM((blocks, 2 * LANE, LANE), BF16),
            pltpu.VMEM((blocks, depth, side, LANE), F32),
            pltpu.VMEM((blocks, cells, LANE), F32),
            pltpu.VMEM((blocks, walls, LANE), F32),
            pltpu.VMEM((cells, width), BF16),
            pltpu.VMEM((cells, width), BF16),
            pltpu.VMEM((LANE, width), BF16),
            pltpu.VMEM((blocks, LANE, 3 * LANE), BF16),
            pltpu.VMEM((nvel, MOM, cells), F32),
            pltpu.VMEM((LANE, cells), F32),
            pltpu.VMEM((cells, LANE), BF16),
            pltpu.VMEM((cells, LANE), F32),
            pltpu.VMEM((cells, LANE), F32),
            pltpu.VMEM((8, cells), F32),
            pltpu.VMEM((8, cells), F32),
            pltpu.VMEM((blocks, depth, side, LANE), F32),
            pltpu.VMEM((blocks, depth, side, LANE), F32),
            pltpu.VMEM(face, F32),
            pltpu.VMEM((half, 2, side, LANE), F32),
            pltpu.VMEM(face, F32),
            pltpu.VMEM(face, F32),
            pltpu.VMEM(face, F32),
            pltpu.VMEM(face, F32),
            pltpu.VMEM(face, F32),
            pltpu.VMEM(face, F32),
            pltpu.VMEM(face, F32),
            pltpu.VMEM(face, F32),
            pltpu.SemaphoreType.DMA,
            pltpu.SemaphoreType.DMA((nvel - 1,)),
            pltpu.SemaphoreType.DMA((nvel - 1,)),
            pltpu.SemaphoreType.DMA((nvel - 1,)),
            pltpu.SemaphoreType.DMA((nvel - 1,)),
            pltpu.SemaphoreType.DMA((2,)),
        ]
        + [pltpu.SemaphoreType.DMA((half, planes))] * 8,
        compiler_params=pltpu.CompilerParams(
            collective_id=0, has_side_effects=True, vmem_limit_bytes=62 * 1024 * 1024
        ),
    )(wall_mask.transpose(1, 2, 0), grid_point.reshape(blocks, LANE), mirror_slot.reshape(blocks, LANE), flat)
    return (
        out.reshape(depth, rows, blocks, planes, LANE)
        .transpose(0, 1, 3, 2, 4)
        .reshape(depth, rows, planes, width)
    )


def solution(mesh):
    placed = (P("space", None, None, "vel"), P("space", None, None), P("vel"), P("vel"))
    body = functools.partial(shards, mesh.shape["space"], mesh.shape["vel"])
    return jax.shard_map(
        body, mesh=mesh, in_specs=placed, out_specs=P("space", None, None, "vel"), check_vma=False
    )
```

```python
import functools
import math

import jax
import jax.numpy as jnp
from jax import lax
from jax.experimental import pallas as pl
from jax.experimental.pallas import tpu as pltpu
from jax.sharding import PartitionSpec as P

VS = 16
LANE = 128
FEAT = 8
MOM = 16
MESH = pl.DeviceIdType.MESH

stream_x = 40.0
stream_y = 0.15
stream_z = 0.05
relaxation_multiplier = 0.05
shear_power_index = 0.81
diffusivity_ratio = 2.0 / 3.0

F32 = jnp.float32
BF16 = jnp.bfloat16


def rounded(x):
    return x.astype(BF16).astype(F32)


def velocity_rows(points):
    spacing = 8.0 / VS
    half = (VS - 1) / 2.0
    bits = VS.bit_length() - 1
    first = lax.shift_right_logical(points, 2 * bits).astype(F32)
    second = (lax.shift_right_logical(points, bits) & (VS - 1)).astype(F32)
    third = (points & (VS - 1)).astype(F32)
    return [(v - half) * spacing for v in (first, second, third)]


def stacked(rows, height):
    index = lax.broadcasted_iota(jnp.int32, (height, LANE), 0)
    out = jnp.zeros((height, LANE), F32)
    for k, row in enumerate(rows):
        out = jnp.where(index == k, row, out)
    return out


def kernel(
    dims,
    wall_mask,
    grid_ref,
    mirror_ref,
    f_ref,
    out_ref,
    wall_ref,
    wsplit_ref,
    pick_ref,
    cell_ref,
    eq_ref,
    mirrored_ref,
    fhi_ref,
    flo_ref,
    tmom_ref,
    gmat_ref,
    mom_ref,
    coef_ref,
    lhs_ref,
    rate_ref,
    prate_ref,
    rate_send,
    rate_recv,
    sa_ref,
    sb_ref,
    pb_ref,
    pair_a,
    pair_b,
    ed_ref,
    eu_ref,
    od_ref,
    ou_ref,
    enter_own,
    enter_send,
    enter_recv,
    wall_ssem,
    wall_rsem,
    mom_ssem,
    mom_rsem,
    rate_sem,
    face_ssem,
    face_rsem,
    dn_ssem,
    dn_rsem,
    up_ssem,
    up_rsem,
    ret_ssem,
    ret_rsem,
):
    depth, rows, planes, blocks, nspace, nvel = dims
    stride = blocks * planes
    cells_x = planes * rows
    cells = depth * cells_x
    walls = depth * 2 * planes
    half_blocks = blocks // 2
    pairs = nspace // 2
    weight = (8.0 / VS) ** 3

    s = lax.axis_index("space")
    v = lax.axis_index("vel")
    q = lax.rem(s, 2)
    p = lax.div(s, 2)
    partner = s + 1 - 2 * q
    own0 = q * half_blocks
    far0 = (1 - q) * half_blocks

    def frow(x, y, j, z):
        return (x * rows + y) * stride + j * planes + z

    barrier = pltpu.get_barrier_semaphore()
    for d in range(1, nvel):
        pl.semaphore_signal(
            barrier, inc=1, device_id=(s, lax.rem(v + d, nvel)), device_id_type=MESH
        )
    pl.semaphore_signal(barrier, inc=1, device_id=(partner, v), device_id_type=MESH)

    @pl.when(p > 0)
    def _():
        pl.semaphore_signal(barrier, inc=1, device_id=(s - 2, v), device_id_type=MESH)

    @pl.when(p < pairs - 1)
    def _():
        pl.semaphore_signal(barrier, inc=1, device_id=(s + 2, v), device_id_type=MESH)

    tmom_ref[...] = jnp.zeros_like(tmom_ref)
    gmat_ref[...] = jnp.zeros_like(gmat_ref)
    coef_ref[...] = jnp.zeros_like(coef_ref)
    for j in range(blocks):
        x1, x2, x3 = velocity_rows(grid_ref[j : j + 1, :])
        one = jnp.ones_like(x1)
        square = x1 * x1 + x2 * x2 + x3 * x3
        cubic = [x * square for x in (x1, x2, x3)]
        cubic_hi = [rounded(x) for x in cubic]
        cubic_lo = [x - h for x, h in zip(cubic, cubic_hi)]
        table = [one, x1, x2, x3, x1 * x1, x2 * x2, x3 * x3, x1 * x2, x1 * x3, x2 * x3]
        tmom_ref[0:MOM, j * LANE : (j + 1) * LANE] = stacked(
            table + cubic_hi + cubic_lo, MOM
        ).astype(BF16)
        feat = stacked(table[:7], FEAT)
        zero = jnp.zeros_like(feat)
        for g in range(3):
            column = [zero] * 9
            for part in range(3):
                column[3 * part + g] = feat
            column = column + [zero]
            gmat_ref[j, 0 : 10 * FEAT, g * LANE : (g + 1) * LANE] = jnp.concatenate(
                column, axis=0
            ).astype(BF16)

        slot = mirror_ref[j : j + 1, :]
        index = lax.broadcasted_iota(jnp.int32, (2 * LANE, LANE), 0) & (LANE - 1)
        pick_ref[j] = jnp.where(index == (slot & (LANE - 1)), 1.0, 0.0).astype(BF16)

    for x in range(depth):
        for w in range(2):
            for z in range(planes):
                r = (x * 2 + w) * planes + z
                y = (rows - 1) * w
                wall_ref[v, pl.ds(r, blocks, stride=walls), :] = f_ref[
                    pl.ds(frow(x, y, 0, z), blocks, stride=planes), :
                ]

    for x in range(depth):
        for z in range(planes):
            base = (x * planes + z) * rows
            for j in range(blocks):
                part = f_ref[pl.ds(frow(x, 0, j, z), rows, stride=stride), :]
                hi = part.astype(BF16)
                lo = (part - hi.astype(F32)).astype(BF16)
                cell_ref[j, x, z * rows : (z + 1) * rows, :] = part
                fhi_ref[base : base + rows, j * LANE : (j + 1) * LANE] = hi
                flo_ref[base : base + rows, j * LANE : (j + 1) * LANE] = lo

    greetings = nvel + (p > 0).astype(jnp.int32) + (p < pairs - 1).astype(jnp.int32)
    pl.semaphore_wait(barrier, greetings)

    sibling = v + 1 - 2 * lax.rem(v, 2)
    twins = nvel // 2

    def far(base, m):
        return lax.rem(base + 2 * m + nvel, nvel)

    def wall_copy(k, origin, target):
        return pltpu.make_async_remote_copy(
            src_ref=wall_ref.at[origin],
            dst_ref=wall_ref.at[origin],
            send_sem=wall_ssem.at[k],
            recv_sem=wall_rsem.at[k],
            device_id=(s, target),
            device_id_type=MESH,
        )

    def wall_far(m):
        return wall_copy(m, v, far(v, m))

    def wall_far_arrival(m):
        return wall_copy(m, far(v, -m), far(v, m))

    def wall_forward(m):
        return wall_copy(twins - 1 + m, far(v, -m), sibling)

    def wall_forward_arrival(m):
        return wall_copy(twins - 1 + m, far(sibling, -m), sibling)

    def mom_copy(k):
        target = far(v if k % 2 == 0 else sibling, k // 2)
        return pltpu.make_async_remote_copy(
            src_ref=mom_ref.at[0],
            dst_ref=mom_ref.at[k],
            send_sem=mom_ssem.at[k - 1],
            recv_sem=mom_rsem.at[k - 1],
            device_id=(s, target),
            device_id_type=MESH,
        )

    for m in range(1, twins):
        wall_far(m).start()
    wall_copy(0, v, sibling).start()

    contract = (((1,), (1,)), ((), ()))
    sums = lax.dot_general(
        fhi_ref[...], tmom_ref[...], contract, preferred_element_type=F32
    ) + lax.dot_general(flo_ref[...], tmom_ref[...], contract, preferred_element_type=F32)
    mom_ref[0] = sums.T[0:MOM, :]
    for d in range(nvel - 1, 0, -1):
        mom_copy(d).start()
    for m in range(1, twins):
        wall_far_arrival(m).wait_recv()
        wall_forward(m).start()
    row_index = lax.broadcasted_iota(jnp.int32, (rows, LANE), 0)

    def block_tables(j):
        return velocity_rows(grid_ref[pl.ds(j, 1), :])

    def flux_block(j, carry):
        _, x2, x3 = block_tables(j)
        pos2 = x2 > 0
        pos3 = x3 > 0
        coef_y = stream_y * jnp.abs(x2)
        coef_z = stream_z * jnp.abs(x3)
        coef_f = 1.0 - coef_y - coef_z
        for x in range(depth):
            values = [
                cell_ref[j, x, z * rows : (z + 1) * rows, :] for z in range(planes)
            ]
            for z in range(planes):
                below = jnp.where(row_index == 0, 0.0, pltpu.roll(values[z], 1, axis=0))
                above = jnp.where(
                    row_index == rows - 1, 0.0, pltpu.roll(values[z], rows - 1, axis=0)
                )
                side = jnp.where(pos2, below, above)
                before, after = values[(z - 1) % planes], values[(z + 1) % planes]
                if (z - 1) % planes == (z + 1) % planes:
                    plane = before
                else:
                    plane = jnp.where(pos3, before, after)
                sb_ref[j, x, z * rows : (z + 1) * rows, :] = (
                    coef_f * values[z] + coef_y * side + coef_z * plane
                )
        return carry

    lax.fori_loop(0, blocks, flux_block, 0)

    total = mom_ref[0]
    for d in range(1, nvel):
        mom_copy(d).wait_recv()
        total = total + mom_ref[d]
    total = total * weight

    raw = [total[k : k + 1, :] for k in range(MOM)]
    density = raw[0]
    momentum = raw[1:4]
    flow = [m / density for m in momentum]
    tensor = [[raw[4], raw[7], raw[8]], [raw[7], raw[5], raw[9]], [raw[8], raw[9], raw[6]]]
    third = [raw[10 + k] + raw[13 + k] for k in range(3)]
    trace = raw[4] + raw[5] + raw[6]
    flow_sq = flow[0] * flow[0] + flow[1] * flow[1] + flow[2] * flow[2]
    temperature = (trace - density * flow_sq) / (3.0 * density)
    flow_mom = flow[0] * momentum[0] + flow[1] * momentum[1] + flow[2] * momentum[2]
    heat = []
    for k in range(3):
        contracted = flow[0] * tensor[k][0] + flow[1] * tensor[k][1] + flow[2] * tensor[k][2]
        heat.append(
            0.5
            * (
                third[k]
                - 2.0 * contracted
                + flow_sq * momentum[k]
                - flow[k] * trace
                + 2.0 * flow[k] * flow_mom
                - flow[k] * flow_sq * density
            )
        )
    log_t = jnp.log(temperature)
    inverse_t = 1.0 / temperature
    rate = relaxation_multiplier * density * jnp.exp((1.0 - shear_power_index) * log_t)

    rate_send[...] = jnp.broadcast_to(rate, rate_send.shape)

    def rate_copy():
        return pltpu.make_async_remote_copy(
            src_ref=rate_send,
            dst_ref=rate_recv,
            send_sem=rate_sem.at[0],
            recv_sem=rate_sem.at[1],
            device_id=(partner, v),
            device_id_type=MESH,
        )

    rate_copy().start()
    scale = (1.0 - diffusivity_ratio) / 5.0 * inverse_t * inverse_t / density
    flow_heat = flow[0] * heat[0] + flow[1] * heat[1] + flow[2] * heat[2]
    exponent = [
        jnp.log(density) - 1.5 * (log_t + math.log(2.0 * math.pi)) - 0.5 * flow_sq * inverse_t
    ]
    exponent += [u * inverse_t for u in flow] + [-0.5 * inverse_t] * 3
    linear = [-scale * flow_heat] + [scale * h for h in heat]
    bracket = [flow_sq * inverse_t - 5.0]
    bracket += [-2.0 * u * inverse_t for u in flow] + [inverse_t] * 3
    for g, group in enumerate((exponent, linear, bracket)):
        for k, row in enumerate(group):
            coef_ref[g * FEAT + k : g * FEAT + k + 1, :] = row
    whole = coef_ref[0 : 3 * FEAT, :]
    hi = rounded(whole)
    mid = rounded(whole - hi)
    coef_ref[0 : 3 * FEAT, :] = hi
    coef_ref[3 * FEAT : 6 * FEAT, :] = mid
    coef_ref[6 * FEAT : 9 * FEAT, :] = whole - hi - mid
    lhs_ref[...] = coef_ref[...].T.astype(BF16)
    rate_ref[...] = jnp.broadcast_to(rate, (LANE, cells)).T

    for j in range(blocks):
        got = jnp.dot(lhs_ref[...], gmat_ref[j], preferred_element_type=F32)
        eq_ref[j] = jnp.exp(got[:, :LANE]) * (
            1.0 + got[:, LANE : 2 * LANE] * got[:, 2 * LANE :]
        )

    wall_copy(0, sibling, sibling).wait_recv()
    for m in range(1, twins):
        wall_forward_arrival(m).wait_recv()
    everywhere = wall_ref[...].reshape(nvel * blocks * walls, LANE)
    whi = everywhere.astype(BF16)
    wsplit_ref[:, :LANE] = whi
    wsplit_ref[:, LANE:] = (everywhere - whi.astype(F32)).astype(BF16)
    for j in range(blocks):
        high = lax.shift_right_logical(mirror_ref[j : j + 1, :], LANE.bit_length() - 1)
        found = jnp.dot(wsplit_ref[...], pick_ref[j], preferred_element_type=F32)
        acc = jnp.zeros((walls, LANE), F32)
        for h in range(nvel * blocks):
            acc = acc + jnp.where(high == h, found[h * walls : (h + 1) * walls], 0.0)
        mirrored_ref[j] = acc

    first_edge = jnp.where(s == 0, 1.0, 0.0).astype(F32)
    last_edge = jnp.where(s == nspace - 1, 1.0, 0.0).astype(F32)
    def local_block(j):
        x1, x2, _ = block_tables(j)
        pos1 = x1 > 0
        pos2 = x2 > 0
        coef_y = stream_y * jnp.abs(x2)
        coef_low = jnp.where(pos2, coef_y, 0.0)
        coef_high = jnp.where(pos2, 0.0, coef_y)
        sigma = stream_x * jnp.abs(x1)
        opening = 1.0 + sigma
        edge = jnp.where(pos1, first_edge, last_edge)
        mirrored = mirrored_ref[j]
        group_index = lax.broadcasted_iota(jnp.int32, (8, LANE), 0)
        a_list, b_list, eq_list = [], [], []
        for x in range(depth):
            base = x * cells_x
            equilibrium = eq_ref[j, base : base + cells_x, :]
            rates = rate_ref[base : base + cells_x, :]
            inverse = 1.0 / (opening + rates)
            parts = []
            for z in range(planes):
                low = (x * 2) * planes + z
                high = (x * 2 + 1) * planes + z
                mask_low = jnp.full((1, LANE), wall_mask[x, 0, z])
                mask_high = jnp.full((1, LANE), wall_mask[x, 1, z])
                eq_z = equilibrium[z * rows : (z + 1) * rows]
                ghost_low = jnp.where(mask_low == 1, mirrored[low : low + 1], eq_z[0:1])
                ghost_high = jnp.where(
                    mask_high == 1, mirrored[high : high + 1], eq_z[rows - 1 : rows]
                )
                flux = sb_ref[j, x, z * rows : (z + 1) * rows, :]
                parts += [
                    flux[:8] + jnp.where(group_index == 0, coef_low * ghost_low, 0.0),
                    flux[8 : rows - 8],
                    flux[rows - 8 :] + jnp.where(group_index == 7, coef_high * ghost_high, 0.0),
                ]
            b_list.append((jnp.concatenate(parts, axis=0) + rates * equilibrium) * inverse)
            a_list.append(sigma * inverse)
            if x in (0, depth - 1):
                eq_list.append(equilibrium)
        a_run = b_run = None
        for k in range(depth):
            a_k = jnp.where(pos1, a_list[k], a_list[depth - 1 - k])
            b_k = jnp.where(pos1, b_list[k], b_list[depth - 1 - k])
            if k == 0:
                target = jnp.where(pos1, eq_list[0], eq_list[-1])
                b_run = b_k + a_k * (edge * target)
                a_run = a_k * (1.0 - edge)
            else:
                b_run = a_k * b_run + b_k
                a_run = a_k * a_run
            sa_ref[j, k] = a_run
            sb_ref[j, k] = b_run

    def band(z):
        return pl.ds(z * rows, rows)

    def face_copy(c, z):
        return pltpu.make_async_remote_copy(
            src_ref=sb_ref.at[far0 + c, depth - 1, band(z)],
            dst_ref=pb_ref.at[c, band(z)],
            send_sem=face_ssem.at[c, z],
            recv_sem=face_rsem.at[c, z],
            device_id=(partner, v),
            device_id_type=MESH,
        )

    def far_block(c, carry):
        local_block(far0 + c)
        for z in range(planes):
            face_copy(c, z).start()
        return carry

    lax.fori_loop(0, half_blocks, far_block, 0)

    rate_copy().wait()
    prate_ref[...] = jnp.broadcast_to(rate_recv[0:1, :], (LANE, cells)).T


    def first_weight(x1):
        sign = jnp.where(x1 > 0, 1.0, -1.0)
        return sign * jnp.where(q == 0, 1.0, -1.0) > 0

    def pair_block(c):
        j = own0 + c
        local_block(j)
        x1, _, _ = block_tables(j)
        sigma = stream_x * jnp.abs(x1)
        opening = 1.0 + sigma
        other = None
        for x in range(depth):
            a = sigma / (opening + prate_ref[x * cells_x : (x + 1) * cells_x, :])
            other = a if other is None else other * a
        for z in range(planes):
            face_copy(c, z).wait_recv()
        a_own = sa_ref[j, depth - 1]
        b_own = sb_ref[j, depth - 1]
        b_other = pb_ref[c]
        first = first_weight(x1)
        pair_a[c, 0] = other
        pair_a[c, 1] = a_own * other
        pair_b[c] = jnp.where(first, other * b_own + b_other, a_own * b_other + b_own)

    def down_copy(c, z):
        return pltpu.make_async_remote_copy(
            src_ref=od_ref.at[c, band(z)],
            dst_ref=ed_ref.at[c, band(z)],
            send_sem=dn_ssem.at[c, z],
            recv_sem=dn_rsem.at[c, z],
            device_id=(s + 2, v),
            device_id_type=MESH,
        )

    def up_copy(c, z):
        return pltpu.make_async_remote_copy(
            src_ref=ou_ref.at[c, band(z)],
            dst_ref=eu_ref.at[c, band(z)],
            send_sem=up_ssem.at[c, z],
            recv_sem=up_rsem.at[c, z],
            device_id=(s - 2, v),
            device_id_type=MESH,
        )

    def return_copy(c, z):
        return pltpu.make_async_remote_copy(
            src_ref=enter_send.at[c, band(z)],
            dst_ref=enter_recv.at[c, band(z)],
            send_sem=ret_ssem.at[c, z],
            recv_sem=ret_rsem.at[c, z],
            device_id=(partner, v),
            device_id_type=MESH,
        )

    @pl.when(p == 0)
    def _():
        ed_ref[...] = jnp.zeros_like(ed_ref)

    @pl.when(p == pairs - 1)
    def _():
        eu_ref[...] = jnp.zeros_like(eu_ref)

    def finish(j, enter):
        x1, _, _ = block_tables(j)
        pos1 = x1 > 0
        done = [sa_ref[j, k] * enter + sb_ref[j, k] for k in range(depth)]
        for x in range(depth):
            value = jnp.where(pos1, done[x], done[depth - 1 - x])
            for z in range(planes):
                out_ref[pl.ds(frow(x, 0, j, z), rows, stride=stride), :] = value[
                    z * rows : (z + 1) * rows
                ]

    back = pairs - 1 - p
    latest = jnp.maximum(p, back)

    def chain_step(t, carry):
        c_dn = t - p
        c_up = t - back
        c_end = t - latest

        @pl.when(t < half_blocks)
        def _():
            pair_block(t)

        @pl.when((c_dn >= 0) & (c_dn < half_blocks))
        def _():
            for z in range(planes):
                at = (c_dn, band(z))

                @pl.when(p > 0)
                def _():
                    down_copy(c_dn, z).wait_recv()

                @pl.when(p < pairs - 1)
                def _():
                    od_ref[at] = pair_a[c_dn, 1, band(z)] * ed_ref[at] + pair_b[at]
                    down_copy(c_dn, z).start()

        @pl.when((c_up >= 0) & (c_up < half_blocks))
        def _():
            for z in range(planes):
                at = (c_up, band(z))

                @pl.when(p < pairs - 1)
                def _():
                    up_copy(c_up, z).wait_recv()

                @pl.when(p > 0)
                def _():
                    ou_ref[at] = pair_a[c_up, 1, band(z)] * eu_ref[at] + pair_b[at]
                    up_copy(c_up, z).start()

        @pl.when((c_end >= 0) & (c_end < half_blocks))
        def _():
            j = own0 + c_end
            x1, _, _ = block_tables(j)
            first = first_weight(x1)
            for z in range(planes):
                at = (c_end, band(z))
                enter = jnp.where(x1 > 0, ed_ref[at], eu_ref[at])
                last = (j, depth - 1, band(z))
                after_own = sa_ref[last] * enter + sb_ref[last]
                after_other = pair_a[c_end, 0, band(z)] * enter + pb_ref[at]
                enter_send[at] = jnp.where(first, after_own, enter)
                return_copy(c_end, z).start()
                enter_own[at] = jnp.where(first, enter, after_other)
            finish(j, enter_own[c_end])

        return carry

    lax.fori_loop(0, half_blocks + pairs - 1, chain_step, 0)

    def finish_far(c, carry):
        for z in range(planes):
            return_copy(c, z).wait_recv()
        finish(far0 + c, enter_recv[c])
        return carry

    lax.fori_loop(0, half_blocks, finish_far, 0)

    wall_copy(0, v, sibling).wait_send()
    for m in range(1, twins):
        wall_far(m).wait_send()
        wall_forward(m).wait_send()
    for d in range(1, nvel):
        mom_copy(d).wait_send()

    def drain(c, carry):
        for z in range(planes):
            face_copy(c, z).wait_send()
            return_copy(c, z).wait_send()

            @pl.when(p < pairs - 1)
            def _():
                down_copy(c, z).wait_send()

            @pl.when(p > 0)
            def _():
                up_copy(c, z).wait_send()

        return carry

    lax.fori_loop(0, half_blocks, drain, 0)


def shards(nspace, nvel, distribution, wall_mask, grid_point, mirror_slot):
    depth, rows, planes, width = distribution.shape
    blocks = width // LANE
    half = blocks // 2
    dims = (depth, rows, planes, blocks, nspace, nvel)
    count = depth * rows * planes * blocks
    stride = blocks * planes
    side = planes * rows
    cells = depth * side
    walls = depth * 2 * planes
    flat = (
        distribution.reshape(depth, rows, planes, blocks, LANE)
        .transpose(0, 1, 3, 2, 4)
        .reshape(count, LANE)
    )
    vmem = pl.BlockSpec(memory_space=pltpu.VMEM)
    face = (half, side, LANE)
    out = pl.pallas_call(
        functools.partial(kernel, dims),
        out_shape=jax.ShapeDtypeStruct((count, LANE), F32),
        in_specs=[
            pl.BlockSpec(memory_space=pltpu.SMEM),
            vmem,
            vmem,
            vmem,
        ],
        out_specs=vmem,
        scratch_shapes=[
            pltpu.VMEM((nvel, blocks * walls, LANE), F32),
            pltpu.VMEM((nvel * blocks * walls, 2 * LANE), BF16),
            pltpu.VMEM((blocks, 2 * LANE, LANE), BF16),
            pltpu.VMEM((blocks, depth, side, LANE), F32),
            pltpu.VMEM((blocks, cells, LANE), F32),
            pltpu.VMEM((blocks, walls, LANE), F32),
            pltpu.VMEM((cells, width), BF16),
            pltpu.VMEM((cells, width), BF16),
            pltpu.VMEM((LANE, width), BF16),
            pltpu.VMEM((blocks, LANE, 3 * LANE), BF16),
            pltpu.VMEM((nvel, MOM, cells), F32),
            pltpu.VMEM((LANE, cells), F32),
            pltpu.VMEM((cells, LANE), BF16),
            pltpu.VMEM((cells, LANE), F32),
            pltpu.VMEM((cells, LANE), F32),
            pltpu.VMEM((8, cells), F32),
            pltpu.VMEM((8, cells), F32),
            pltpu.VMEM((blocks, depth, side, LANE), F32),
            pltpu.VMEM((blocks, depth, side, LANE), F32),
            pltpu.VMEM(face, F32),
            pltpu.VMEM((half, 2, side, LANE), F32),
            pltpu.VMEM(face, F32),
            pltpu.VMEM(face, F32),
            pltpu.VMEM(face, F32),
            pltpu.VMEM(face, F32),
            pltpu.VMEM(face, F32),
            pltpu.VMEM(face, F32),
            pltpu.VMEM(face, F32),
            pltpu.VMEM(face, F32),
            pltpu.SemaphoreType.DMA((nvel - 1,)),
            pltpu.SemaphoreType.DMA((nvel - 1,)),
            pltpu.SemaphoreType.DMA((nvel - 1,)),
            pltpu.SemaphoreType.DMA((nvel - 1,)),
            pltpu.SemaphoreType.DMA((2,)),
        ]
        + [pltpu.SemaphoreType.DMA((half, planes))] * 8,
        compiler_params=pltpu.CompilerParams(
            collective_id=0, has_side_effects=True, vmem_limit_bytes=40 * 1024 * 1024
        ),
    )(wall_mask, grid_point.reshape(blocks, LANE), mirror_slot.reshape(blocks, LANE), flat)
    return (
        out.reshape(depth, rows, blocks, planes, LANE)
        .transpose(0, 1, 3, 2, 4)
        .reshape(depth, rows, planes, width)
    )


def solution(mesh):
    placed = (P("space", None, None, "vel"), P("space", None, None), P("vel"), P("vel"))
    body = functools.partial(shards, mesh.shape["space"], mesh.shape["vel"])
    return jax.shard_map(
        body, mesh=mesh, in_specs=placed, out_specs=P("space", None, None, "vel"), check_vma=False
    )
```
